128 devices in a mesh: gx: 16 (over x, y), gy: 8 (over z, core).
Axes of the slice: x: 4, y: 4, z: 4, core: 2. Of those that a mesh axis runs over, the one named last changes fastest.
Arguments:
- fine_nodes: bfloat16 [64, 16, 128, 512], P('gx', 'gy'), may hold values from -6 to 6
- edge_states: bfloat16 [16, 8, 64, 128, 512], P('gx', 'gy'), may hold values from -6 to 6
- middle_nodes: bfloat16 [16, 8, 128, 512], P('gx', 'gy'), may hold values from -6 to 6
- coarse_nodes: bfloat16 [1024, 512], P(('gx', 'gy')), may hold values from -6 to 6
- edge_sources: int32 [16, 8, 64, 128], P('gx', 'gy'), may hold values from 0 to 3071, as said below
- target_blocks: int32 [16, 8, 64], P('gx', 'gy'), may hold values from 0 to 7
- target_nodes: int32 [16, 8, 64, 128], P('gx', 'gy'), may hold values from 0 to 127
- live_blocks: int32 [16, 8], P('gx', 'gy'), may hold values from 32 to 64, as said below
- fine_parent: int32 [64, 16, 128], P('gx', 'gy'), may hold values from 0 to 127
- fine_weight: float32 [64, 16, 128], P('gx', 'gy'), may hold values from 0.2 to 0.6
- middle_parent: int32 [16, 8, 128], P('gx', 'gy'), may hold values from 0 to 1023, as said below
- middle_weight: float32 [16, 8, 128], P('gx', 'gy'), may hold values from 0.1 to 0.3
- edge_in: bfloat16 [3, 512, 512], replicated, may hold values from -0.15625 to 0.15625
- edge_bias: float32 [512], replicated, may hold values from -3 to 3
- edge_out: bfloat16 [512, 512], replicated, may hold values from -0.25 to 0.25
- edge_bias_two: float32 [512], replicated, may hold values from -3 to 3
- edge_gain: float32 [512], replicated, may hold values from 0.1 to 1.9
- node_in: bfloat16 [2, 512, 512], replicated, may hold values from -0.1875 to 0.1875
- node_bias: float32 [512], replicated, may hold values from -3 to 3
- node_out: bfloat16 [512, 512], replicated, may hold values from -0.25 to 0.25
- node_bias_two: float32 [512], replicated, may hold values from -3 to 3
- node_gain: float32 [512], replicated, may hold values from 0.1 to 1.9
- coarse_in: bfloat16 [2, 512, 512], replicated, may hold values from -0.1875 to 0.1875
- coarse_bias: float32 [512], replicated, may hold values from -3 to 3
- coarse_out: bfloat16 [512, 512], replicated, may hold values from -0.25 to 0.25
- coarse_bias_two: float32 [512], replicated, may hold values from -3 to 3
- coarse_gain: float32 [512], replicated, may hold values from 0.1 to 1.9
Outputs:
- fine_result: bfloat16 [64, 16, 128, 512], P('gx', 'gy')
- edge_result: bfloat16 [16, 8, 64, 128, 512], P('gx', 'gy')
- middle_result: bfloat16 [16, 8, 128, 512], P('gx', 'gy')
- coarse_result: bfloat16 [1024, 512], P(('gx', 'gy'))
The draws below stay inside these ranges and needn't reach their ends.
Inputs may be any that keep to these rules, and one draw needn't show every extreme that they name: `edge_sources`: sources lie in the device's own blocks or in the blocks touching them (diagonals too), never outside the grid. `live_blocks`: some device has all 64 slots live in every draw. `middle_parent`: coarse node c is owned by device c // 8 in the order of gx+gy. Of the 128 middle nodes of one device, exactly 1 have their parent among the coarse nodes of each owner.
All inputs are finite; a program needn't handle non-finite values.
Results may differ from the reference program's by a relative error of at most 0.0075.
Values may be sent and summed in bfloat16 or wider, within the bound.
No kernel may reach another device: no remote copies, remote signals or barrier semaphores. Data moves between devices by JAX's collectives and lax.ppermute only.
A program may use at most 192 MiB of HBM per device.

```python
import jax
import jax.numpy as jnp
from jax import lax

D = 512
BLK = 128
BX = 4
BY = 2
EB = 64
CO_DEV = 8
MID_DEV = 128
NC = 1024
CAP = 1
N_GX = 16
N_GY = 8


def draw_edge_sources(key, part):
    full_shape = (N_GX, N_GY, EB, BLK)
    horizontal_position = lax.broadcasted_iota(jnp.int32, full_shape, 0)
    along_y = lax.broadcasted_iota(jnp.int32, full_shape, 1)
    low_x = jnp.where(horizontal_position == 0, 1, 0)
    high_x = jnp.where(horizontal_position == N_GX - 1, BX + 1, BX + 2)
    low_y = jnp.where(along_y == 0, 1, 0)
    high_y = jnp.where(along_y == N_GY - 1, BY + 1, BY + 2)
    subkeys = jax.random.split(jax.random.fold_in(key, 11), 3)
    block_x = jax.random.randint(subkeys[0], full_shape, low_x, high_x)
    block_y = jax.random.randint(subkeys[1], full_shape, low_y, high_y)
    node_index = jax.random.randint(subkeys[2], full_shape, 0, BLK)
    return ((block_x * (BY + 2) + block_y) * BLK + node_index).astype(jnp.int32)


def draw_live_blocks(key, part):
    subkeys = jax.random.split(jax.random.fold_in(key, 23), 2)
    counts = jax.random.randint(subkeys[0], (N_GX * N_GY,), EB // 2, EB + 1)
    busiest = jax.random.randint(subkeys[1], (), 0, N_GX * N_GY)
    counts = jnp.where(jnp.arange(N_GX * N_GY) == busiest, EB, counts)
    return counts.reshape(N_GX, N_GY).astype(jnp.int32)


def draw_middle_parent(key, part):
    device_total = N_GX * N_GY
    subkeys = jax.random.split(jax.random.fold_in(key, 37), 2)
    device_keys = jax.random.split(subkeys[0], device_total)
    orders = jax.vmap(lambda one_key: jax.random.permutation(one_key, MID_DEV))(device_keys).astype(jnp.int32)
    owners = orders // CAP
    inside_block_mask = jax.random.randint(subkeys[1], (device_total, MID_DEV), 0, CO_DEV)
    return (owners * CO_DEV + inside_block_mask).reshape(N_GX, N_GY, MID_DEV).astype(jnp.int32)


def set_ends(entries, own_key, least, largest):
    longest = entries.shape.index(max(entries.shape))
    spots = []
    for shift in (0, 1):
        where = [jax.random.randint(jax.random.fold_in(own_key, axis), (), 0, length) for axis, length in enumerate(entries.shape)]
        where[longest] = (where[longest] + shift) % entries.shape[longest]
        spots.append(tuple(where))
    return entries.at[spots[0]].set(least).at[spots[1]].set(largest)


def block_levels(rng, shape, pieces, smallest, high):
    factor_of = 1.0
    for position, shards_of in pieces:
        heights = jax.random.uniform(jax.random.fold_in(jax.random.fold_in(rng, 6), position), (shards_of,), jnp.float32, smallest / len(pieces), high / len(pieces))
        factor_of = factor_of * jnp.repeat(jnp.exp(heights), shape[position] // shards_of).reshape((-1,) + (1,) * (len(shape) - 1 - position))
    return factor_of


def noise(stream_key, shape, scale, most, cuts=(), dtype=jnp.bfloat16):
    values = scale * jax.random.normal(stream_key, shape, jnp.float32)
    if cuts:
        values = values * block_levels(stream_key, shape, cuts, -0.22, 0.18)
    return jnp.clip(values, -most, most).astype(dtype)


def setup_inputs(seed: int = 0) -> dict:
    key_list = jax.random.split(jax.random.key(seed), 28)
    return {
        "fine_nodes": noise(key_list[0], (N_GX * BX, N_GY * BY, BLK, D), 1.0, 6.0, ((0, 16), (1, 8))),
        "edge_states": noise(key_list[1], (N_GX, N_GY, EB, BLK, D), 1.0, 6.0, ((0, 16), (1, 8))),
        "middle_nodes": noise(key_list[2], (N_GX, N_GY, MID_DEV, D), 1.0, 6.0, ((0, 16), (1, 8))),
        "coarse_nodes": noise(key_list[3], (NC, D), 1.0, 6.0, ((0, 128),)),
        "edge_sources": draw_edge_sources(jax.random.fold_in(key_list[27], 71), 0),
        "target_blocks": set_ends(jax.random.randint(key_list[5], (N_GX, N_GY, EB), 0, BX * BY), jax.random.fold_in(key_list[5], 1), 0, (BX * BY) - 1).astype(jnp.int32),
        "target_nodes": set_ends(jax.random.randint(key_list[6], (N_GX, N_GY, EB, BLK), 0, BLK), jax.random.fold_in(key_list[6], 1), 0, BLK - 1).astype(jnp.int32),
        "live_blocks": draw_live_blocks(jax.random.fold_in(key_list[27], 71), 0),
        "fine_parent": set_ends(jax.random.randint(key_list[8], (N_GX * BX, N_GY * BY, BLK), 0, MID_DEV), jax.random.fold_in(key_list[8], 1), 0, MID_DEV - 1).astype(jnp.int32),
        "fine_weight": jnp.clip(0.2 + 0.400000021 * jax.random.uniform(key_list[9], (N_GX * BX, N_GY * BY, BLK), jnp.float32) ** block_levels(key_list[9], (N_GX * BX, N_GY * BY, BLK), ((0, 16), (1, 8)), -0.2, 0.2), 0.2, 0.6),
        "middle_parent": draw_middle_parent(jax.random.fold_in(key_list[27], 71), 0),
        "middle_weight": jnp.clip(0.1 + 0.20000001043081284 * jax.random.uniform(key_list[11], (N_GX, N_GY, MID_DEV), jnp.float32) ** block_levels(key_list[11], (N_GX, N_GY, MID_DEV), ((0, 16), (1, 8)), -0.2, 0.2), 0.1, 0.3),
        "edge_in": noise(key_list[12], (3, D, D), (3 * D) ** -0.5, 0.15625),
        "edge_bias": noise(key_list[13], (D,), 0.5, 3.0, (), jnp.float32),
        "edge_out": noise(key_list[14], (D, D), D ** -0.5, 0.25),
        "edge_bias_two": noise(key_list[15], (D,), 0.5, 3.0, (), jnp.float32),
        "edge_gain": jnp.clip(1.0 + 0.18 * jax.random.normal(key_list[16], (D,), jnp.float32), 0.1, 1.9),
        "node_in": noise(key_list[17], (2, D, D), (2 * D) ** -0.5, 0.1875),
        "node_bias": noise(key_list[18], (D,), 0.5, 3.0, (), jnp.float32),
        "node_out": noise(key_list[19], (D, D), D ** -0.5, 0.25),
        "node_bias_two": noise(key_list[20], (D,), 0.5, 3.0, (), jnp.float32),
        "node_gain": jnp.clip(1.0 + 0.18 * jax.random.normal(key_list[21], (D,), jnp.float32), 0.1, 1.9),
        "coarse_in": noise(key_list[22], (2, D, D), (2 * D) ** -0.5, 0.1875),
        "coarse_bias": noise(key_list[23], (D,), 0.5, 3.0, (), jnp.float32),
        "coarse_out": noise(key_list[24], (D, D), D ** -0.5, 0.25),
        "coarse_bias_two": noise(key_list[25], (D,), 0.5, 3.0, (), jnp.float32),
        "coarse_gain": jnp.clip(1.0 + 0.18 * jax.random.normal(key_list[26], (D,), jnp.float32), 0.1, 1.9),
    }


epsilon = 1e-05

def layer_norm(values, gain_vec):
    centred = values - lax.optimization_barrier(jnp.mean(values, axis=-1, keepdims=True))
    spread = lax.optimization_barrier(jnp.mean(centred * centred, axis=-1, keepdims=True))
    return centred * lax.rsqrt(spread + epsilon) * gain_vec

def two_layer(pre_act, bias_one, second_weight, bias_two, gain_vec):
    hidden = jax.nn.silu(pre_act + bias_one).astype(jnp.bfloat16)
    output = jnp.dot(hidden, second_weight, preferred_element_type=jnp.float32) + bias_two
    return layer_norm(output, gain_vec)

def to_devices(array):
    tail = array.shape[3:]
    shaped = array.reshape((N_GX, BX, N_GY, BY) + array.shape[2:])
    order = (0, 2, 1, 3) + tuple(range(4, shaped.ndim))
    return shaped.transpose(order).reshape((N_GX * N_GY, BX * BY * BLK) + tail)

def from_devices(array):
    shaped = array.reshape((N_GX, N_GY, BX, BY, BLK) + array.shape[2:])
    order = (0, 2, 1, 3) + tuple(range(4, shaped.ndim))
    return shaped.transpose(order).reshape((N_GX * BX, N_GY * BY, BLK) + array.shape[2:])

def reference(fine_nodes, edge_states, middle_nodes, coarse_nodes, edge_sources, target_blocks, target_nodes, live_blocks, fine_parent, fine_weight, middle_parent, middle_weight, edge_in, edge_bias, edge_out, edge_bias_two, edge_gain, node_in, node_bias, node_out, node_bias_two, node_gain, coarse_in, coarse_bias, coarse_out, coarse_bias_two, coarse_gain):
    device_total = N_GX * N_GY
    own_count = BX * BY * BLK
    padded_all = jnp.pad(fine_nodes, ((1, 1), (1, 1), (0, 0), (0, 0)))
    parents_dev = to_devices(fine_parent)
    weights_dev = to_devices(fine_weight)
    zero_index = jnp.zeros((), jnp.int32)

    def fine_device(inputs):
        device, edge_rows, sources, block_target, node_target, live_count, parents, weights, middle_rows = inputs
        row_x = (device // N_GY).astype(jnp.int32)
        row_y = (device % N_GY).astype(jnp.int32)
        window = lax.dynamic_slice(padded_all, (row_x * BX, row_y * BY, zero_index, zero_index), (BX + 2, BY + 2, BLK, D)).reshape(-1, D)
        own_rows = lax.dynamic_slice(fine_nodes, (row_x * BX, row_y * BY, zero_index, zero_index), (BX, BY, BLK, D)).reshape(own_count, D)
        targets = (block_target[:, None] * BLK + node_target).reshape(-1).astype(jnp.int32)
        flat_edges = edge_rows.reshape(-1, D)
        from_source = jnp.take(window, sources.reshape(-1).astype(jnp.int32), axis=0)
        from_target = jnp.take(own_rows, targets, axis=0)
        pre_act = jnp.dot(flat_edges, edge_in[0], preferred_element_type=jnp.float32)
        pre_act = pre_act + jnp.dot(from_source, edge_in[1], preferred_element_type=jnp.float32)
        pre_act = pre_act + jnp.dot(from_target, edge_in[2], preferred_element_type=jnp.float32)
        message = two_layer(pre_act, edge_bias, edge_out, edge_bias_two, edge_gain).astype(jnp.bfloat16)
        active_block_mask = jnp.broadcast_to((jnp.arange(EB) < live_count)[:, None], (EB, BLK)).reshape(-1, 1)
        message = jnp.where(active_block_mask, message, jnp.zeros_like(message))
        edge_latent_updated = jnp.where(active_block_mask, (flat_edges.astype(jnp.float32) + message.astype(jnp.float32)).astype(jnp.bfloat16), flat_edges)
        aggregate = jax.ops.segment_sum(message.astype(jnp.float32), targets, num_segments=own_count).astype(jnp.bfloat16)
        node_pre = jnp.dot(own_rows, node_in[0], preferred_element_type=jnp.float32)
        node_pre = node_pre + jnp.dot(aggregate, node_in[1], preferred_element_type=jnp.float32)
        fine_mid = own_rows.astype(jnp.float32) + two_layer(node_pre, node_bias, node_out, node_bias_two, node_gain)
        restricted_mid = jax.ops.segment_sum(weights[:, None] * own_rows.astype(jnp.float32), parents.astype(jnp.int32), num_segments=MID_DEV)
        middle_mid = (middle_rows.astype(jnp.float32) + restricted_mid).astype(jnp.bfloat16)
        return (edge_latent_updated.reshape(EB, BLK, D), fine_mid, middle_mid)
    device_ids = jnp.arange(device_total).astype(jnp.int32)
    edge_latent_updated, fine_mid, middle_mid = lax.map(fine_device, (device_ids, edge_states.reshape(device_total, EB, BLK, D), edge_sources.reshape(device_total, EB, BLK), target_blocks.reshape(device_total, EB), target_nodes.reshape(device_total, EB, BLK), live_blocks.reshape(device_total), parents_dev, weights_dev, middle_nodes.reshape(device_total, MID_DEV, D)))
    mid_weights = middle_weight.reshape(device_total, MID_DEV)
    mid_parents = middle_parent.reshape(device_total, MID_DEV).astype(jnp.int32)
    weighted = (mid_weights[:, :, None] * middle_mid.astype(jnp.float32)).reshape(-1, D)
    restricted = jax.ops.segment_sum(weighted, mid_parents.reshape(-1), num_segments=NC).astype(jnp.bfloat16)
    coarse_pre = jnp.dot(coarse_nodes, coarse_in[0], preferred_element_type=jnp.float32)
    coarse_pre = coarse_pre + jnp.dot(restricted, coarse_in[1], preferred_element_type=jnp.float32)
    coarse_result = (coarse_nodes.astype(jnp.float32) + two_layer(coarse_pre, coarse_bias, coarse_out, coarse_bias_two, coarse_gain)).astype(jnp.bfloat16)
    from_coarse = jnp.take(coarse_result, mid_parents, axis=0).astype(jnp.float32)
    middle_result = (middle_mid.astype(jnp.float32) + mid_weights[:, :, None] * from_coarse).astype(jnp.bfloat16)
    from_middle = jnp.take_along_axis(middle_result, parents_dev.astype(jnp.int32)[:, :, None], axis=1).astype(jnp.float32)
    fine_flat = (fine_mid + weights_dev[:, :, None] * from_middle).astype(jnp.bfloat16)
    fine_result = from_devices(fine_flat)
    edge_result = edge_latent_updated.reshape(N_GX, N_GY, EB, BLK, D)
    return (fine_result, edge_result, middle_result.reshape(N_GX, N_GY, MID_DEV, D), coarse_result)
```

```python
import jax
import jax.numpy as jnp
from jax import lax
from jax.sharding import PartitionSpec as P

epsilon = 1e-05


def extended(array, sides, width):
    for axis, dim in sides:
        count, length = (lax.axis_size(axis), array.shape[dim])
        up = [(i, (i + 1) % count) for i in range(count - 1)]
        down = [(j, i) for i, j in up]
        last = lax.slice_in_dim(array, length - width, length, axis=dim)
        first = lax.slice_in_dim(array, 0, width, axis=dim)
        before = lax.ppermute(last, axis, up)
        after = lax.ppermute(first, axis, down)
        array = jnp.concatenate([before, array, after], axis=dim)
    return array


def layer_norm(values, gain_vec):
    centred = values - jnp.mean(values, axis=-1, keepdims=True)
    spread = jnp.mean(centred * centred, axis=-1, keepdims=True)
    return centred * lax.rsqrt(spread + epsilon) * gain_vec


def two_layer(pre_act, bias_one, second_weight, bias_two, gain_vec):
    hidden = jax.nn.silu(pre_act + bias_one).astype(jnp.bfloat16)
    output = jnp.dot(hidden, second_weight, preferred_element_type=jnp.float32) + bias_two
    return layer_norm(output, gain_vec)


def edge_messages(edge_rows, sources, targets, active_block_mask, padded, own_rows, edge_params):
    first_w, bias_one, second_weight, bias_two, gain_vec = edge_params
    latent = edge_rows.shape[-1]
    flat_edges = edge_rows.reshape(-1, latent)
    from_source = jnp.take(padded, sources.reshape(-1), axis=0)
    from_target = jnp.take(own_rows, targets.reshape(-1), axis=0)
    pre_act = jnp.dot(flat_edges, first_w[0], preferred_element_type=jnp.float32)
    pre_act = pre_act + jnp.dot(from_source, first_w[1], preferred_element_type=jnp.float32)
    pre_act = pre_act + jnp.dot(from_target, first_w[2], preferred_element_type=jnp.float32)
    message = two_layer(pre_act, bias_one, second_weight, bias_two, gain_vec).astype(jnp.bfloat16)
    keep_rows = active_block_mask.reshape(-1, 1)
    message = jnp.where(keep_rows, message, jnp.zeros_like(message))
    edge_latent_updated = jnp.where(
        keep_rows,
        (flat_edges.astype(jnp.float32) + message.astype(jnp.float32)).astype(jnp.bfloat16),
        flat_edges,
    )
    return (message.reshape(edge_rows.shape), edge_latent_updated.reshape(edge_rows.shape))


def body(
    fine_nodes,
    edge_states,
    middle_nodes,
    coarse_nodes,
    edge_sources,
    target_blocks,
    target_nodes,
    live_blocks,
    fine_parent,
    fine_weight,
    middle_parent,
    middle_weight,
    edge_in,
    edge_bias,
    edge_out,
    edge_bias_two,
    edge_gain,
    node_in,
    node_bias,
    node_out,
    node_bias_two,
    node_gain,
    coarse_in,
    coarse_bias,
    coarse_out,
    coarse_bias_two,
    coarse_gain,
):
    rows_x, rows_y, block_size, latent = fine_nodes.shape
    own_count = rows_x * rows_y * block_size
    own_rows = fine_nodes.reshape(own_count, latent)
    padded = extended(fine_nodes, (("gx", 0), ("gy", 1)), 1).reshape(-1, latent)
    edge_rows = edge_states[0, 0]
    edge_blocks = edge_rows.shape[0]
    sources = edge_sources[0, 0]
    block_target = target_blocks[0, 0]
    node_target = target_nodes[0, 0]
    targets = block_target[:, None] * block_size + node_target
    live_count = live_blocks[0, 0]
    block_alive = lax.iota(jnp.int32, edge_blocks) < live_count
    active_block_mask = jnp.broadcast_to(block_alive[:, None], (edge_blocks, block_size))
    edge_params = (edge_in, edge_bias, edge_out, edge_bias_two, edge_gain)
    edge_message_rows, edge_latent_updated = edge_messages(
        edge_rows, sources, targets, active_block_mask, padded, own_rows, edge_params
    )
    target_indicator = (
        node_target[:, None, :] == lax.iota(jnp.int32, block_size)[None, :, None]
    ).astype(jnp.bfloat16)
    per_block = jnp.einsum(
        "uot,utx->uox", target_indicator, edge_message_rows, preferred_element_type=jnp.float32
    )
    block_select = (lax.iota(jnp.int32, rows_x * rows_y)[:, None] == block_target[None, :]).astype(
        jnp.float32
    )
    block_sums = jnp.dot(
        block_select,
        per_block.reshape(edge_blocks, block_size * latent),
        precision=lax.Precision.HIGHEST,
        preferred_element_type=jnp.float32,
    )
    aggregate = block_sums.reshape(own_count, latent).astype(jnp.bfloat16)
    node_pre = jnp.dot(own_rows, node_in[0], preferred_element_type=jnp.float32)
    node_pre = node_pre + jnp.dot(aggregate, node_in[1], preferred_element_type=jnp.float32)
    fine_mid = own_rows.astype(jnp.float32) + two_layer(
        node_pre, node_bias, node_out, node_bias_two, node_gain
    )
    parents_local = fine_parent.reshape(own_count)
    weights_local = fine_weight.reshape(own_count)
    middle_rows = middle_nodes[0, 0]
    middle_count = middle_rows.shape[0]
    restrict = (lax.iota(jnp.int32, middle_count)[:, None] == parents_local[None, :]).astype(
        jnp.float32
    ) * weights_local[None, :]
    restricted_mid = jnp.dot(
        restrict,
        own_rows.astype(jnp.float32),
        precision=lax.Precision.HIGHEST,
        preferred_element_type=jnp.float32,
    )
    middle_mid = (middle_rows.astype(jnp.float32) + restricted_mid).astype(jnp.bfloat16)
    mid_parents = middle_parent[0, 0]
    mid_weights = middle_weight[0, 0]
    middle_wide = middle_mid.astype(jnp.float32)
    coarse_own = coarse_nodes.shape[0]
    devices = lax.axis_size(("gx", "gy"))
    owner = mid_parents // coarse_own
    place = mid_parents % coarse_own
    to_owner = lax.iota(jnp.int32, devices)[:, None] == owner[None, :]
    weight_top = lax.reduce_precision(mid_weights, 8, 7)
    weight_middle = lax.reduce_precision(mid_weights - weight_top, 8, 7)
    weight_low = mid_weights - weight_top - weight_middle
    notes = jnp.stack(
        [weight_top, weight_middle, weight_low, place.astype(jnp.float32)], axis=1
    ).astype(jnp.bfloat16)
    notes = jnp.pad(notes, ((0, 0), (0, 124)))
    rows_out = jnp.dot(
        to_owner.astype(jnp.bfloat16),
        jnp.concatenate([middle_mid, notes], axis=1),
        preferred_element_type=jnp.float32,
    ).astype(jnp.bfloat16)
    rows_in = lax.all_to_all(rows_out, ("gx", "gy"), 0, 0, tiled=True)
    notes_in = rows_in[:, latent : latent + 4].astype(jnp.float32)
    weight_in = notes_in[:, 0] + notes_in[:, 1] + notes_in[:, 2]
    place_in = notes_in[:, 3].astype(jnp.int32)
    at_place = lax.iota(jnp.int32, coarse_own)[:, None] == place_in[None, :]
    coarse_summed = jnp.dot(
        at_place.astype(jnp.float32) * weight_in[None, :],
        rows_in[:, :latent].astype(jnp.float32),
        precision=lax.Precision.HIGHEST,
        preferred_element_type=jnp.float32,
    ).astype(jnp.bfloat16)
    coarse_pre = jnp.dot(coarse_nodes, coarse_in[0], preferred_element_type=jnp.float32)
    coarse_pre = coarse_pre + jnp.dot(
        coarse_summed, coarse_in[1], preferred_element_type=jnp.float32
    )
    coarse_result = (
        coarse_nodes.astype(jnp.float32)
        + two_layer(coarse_pre, coarse_bias, coarse_out, coarse_bias_two, coarse_gain)
    ).astype(jnp.bfloat16)
    answers = jnp.dot(
        at_place.T.astype(jnp.bfloat16), coarse_result, preferred_element_type=jnp.float32
    ).astype(jnp.bfloat16)
    from_owners = lax.all_to_all(answers, ("gx", "gy"), 0, 0, tiled=True)
    from_coarse = jnp.dot(
        to_owner.T.astype(jnp.bfloat16), from_owners, preferred_element_type=jnp.float32
    )
    middle_result = (middle_wide + mid_weights[:, None] * from_coarse).astype(jnp.bfloat16)
    from_middle = jnp.take(middle_result, parents_local, axis=0).astype(jnp.float32)
    fine_result = (fine_mid + weights_local[:, None] * from_middle).astype(jnp.bfloat16)
    return (
        fine_result.reshape(fine_nodes.shape),
        edge_latent_updated.reshape(edge_states.shape),
        middle_result.reshape(middle_nodes.shape),
        coarse_result,
    )


def solution(mesh):
    placed = (
        P("gx", "gy", None, None),
        P("gx", "gy", None, None, None),
        P("gx", "gy", None, None),
        P(("gx", "gy"), None),
        P("gx", "gy", None, None),
        P("gx", "gy", None),
        P("gx", "gy", None, None),
        P("gx", "gy"),
        P("gx", "gy", None),
        P("gx", "gy", None),
        P("gx", "gy", None),
        P("gx", "gy", None),
        P(),
        P(),
        P(),
        P(),
        P(),
        P(),
        P(),
        P(),
        P(),
        P(),
        P(),
        P(),
        P(),
        P(),
        P(),
    )
    return jax.shard_map(
        body,
        mesh=mesh,
        in_specs=placed,
        out_specs=(
            P("gx", "gy", None, None),
            P("gx", "gy", None, None, None),
            P("gx", "gy", None, None),
            P(("gx", "gy"), None),
        ),
        check_vma=False,
    )
```

```python
import functools
import jax
import jax.numpy as jnp
from jax import lax
from jax.experimental import pallas as pl
from jax.experimental.pallas import tpu as pltpu
from jax.sharding import PartitionSpec as P

epsilon = 1e-05
SUB = 4
BOTH = ("gx", "gy")


def silu(values):
    half = 0.5 * values
    return half * jnp.tanh(half) + half


def layer_norm(values, gain):
    centred = values - jnp.mean(values, axis=-1, keepdims=True)
    spread = jnp.mean(centred * centred, axis=-1, keepdims=True)
    return centred * lax.rsqrt(spread + epsilon) * gain


def matmul(a, b):
    return jnp.dot(a, b, preferred_element_type=jnp.float32)


def matmul_t(a, b):
    return lax.dot_general(a, b, (((0,), (0,)), ((), ())), preferred_element_type=jnp.float32)


WHOLE = 14


def bring(whole, held, semaphores):
    copies = [pltpu.make_async_copy(a, b, semaphores.at[n]) for n, (a, b) in enumerate(zip(whole, held))]
    for copy in copies:
        copy.start()
    for copy in copies:
        copy.wait()


def edge_kernel(
    edges, *rest
):
    whole, (result, aggregate, table, targets, sums, picked_a, picked_b), held, semaphores = (
        rest[:WHOLE], rest[WHOLE : WHOLE + 7], rest[WHOLE + 7 : -1], rest[-1]
    )
    (sources, target_blocks, live, target_nodes, own, up, down, left, right, first, bias, second, bias_two, gain) = held
    step = pl.program_id(0)
    steps = pl.num_programs(0)
    picked = (picked_a, picked_b)
    latent = own.shape[-1]
    lanes = 128
    parts = latent // lanes
    blk = 128
    chunks = 2 * steps

    def project(piece, places):
        rows = matmul(piece, first[1]) + bias[...]
        for n, place in enumerate(places):
            for j in range(parts):
                table[pl.ds(place * blk * parts + j, blk, stride=parts), :] = rows[
                    n * blk : (n + 1) * blk, j * lanes : (j + 1) * lanes
                ]

    def gather(chunk, b, into):
        block = chunk * SUB + b
        for e in range(blk):
            at = pl.multiple_of(sources[block, e] * parts, parts)
            into[pl.ds((b * blk + e) * parts, parts), :] = table[pl.ds(at, parts), :]

    @pl.when(step == 0)
    def _():
        bring(whole, held, semaphores)
        rows_x, rows_y = own.shape[0], own.shape[1]
        wide = rows_y + 2
        own_rows = own[...].reshape(-1, latent)
        project(own_rows, [(x + 1) * wide + y + 1 for x in range(rows_x) for y in range(rows_y)])
        project(up[...].reshape(-1, latent), [y + 1 for y in range(rows_y)])
        project(down[...].reshape(-1, latent), [(rows_x + 1) * wide + y + 1 for y in range(rows_y)])
        project(left[...].reshape(-1, latent), [x * wide for x in range(rows_x + 2)])
        project(right[...].reshape(-1, latent), [x * wide + wide - 1 for x in range(rows_x + 2)])
        targets[...] = matmul(own_rows, first[2]).astype(jnp.bfloat16).reshape(targets.shape)
        sums[...] = jnp.zeros_like(sums)
        for b in range(SUB):
            gather(0, b, picked_a)

    number = lax.broadcasted_iota(jnp.int32, (blk, blk), 0)

    def compute(half, b_next):
        chunk = 2 * step + half
        ref = picked[half]
        base = half * SUB
        states = edges[base : base + SUB].reshape(SUB * blk, latent)
        pre = matmul(states, first[0])
        hidden = []
        spots = []
        for b in range(SUB):
            b_next(b)
            block = chunk * SUB + b
            to = target_blocks[0, block]
            spot = (target_nodes[pl.ds(block, 1), :] == number).astype(jnp.bfloat16)
            spots.append((to, spot))
            from_target = matmul_t(spot, targets[to])
            from_source = jnp.concatenate(
                [ref[pl.ds(b * blk * parts + j, blk, stride=parts), :] for j in range(parts)], axis=1
            )
            hidden.append(
                silu(pre[b * blk : (b + 1) * blk] + from_target + from_source).astype(jnp.bfloat16)
            )
        out = matmul(jnp.concatenate(hidden, axis=0), second[...]) + bias_two[...]
        for b in range(SUB):
            rows = out[b * blk : (b + 1) * blk]
            block = chunk * SUB + b
            alive = jnp.where(block < live[0, 0], 1.0, 0.0)
            centred = rows - jnp.mean(rows, axis=-1, keepdims=True)
            spread = jnp.mean(centred * centred, axis=-1, keepdims=True)
            message = (centred * (lax.rsqrt(spread + epsilon) * alive) * gain[...]).astype(jnp.bfloat16)
            result[base + b] = edges[base + b] + message
            to, spot = spots[b]
            sums[to] += matmul(spot, message)

    compute(0, lambda b: gather(2 * step + 1, b, picked_b))
    compute(1, lambda b: gather(jnp.minimum(2 * step + 2, chunks - 1), b, picked_a))

    @pl.when(step == steps - 1)
    def _():
        aggregate[...] = sums[...].astype(aggregate.dtype)


def edge_call(edges, *whole):
    count, blk, latent = edges.shape
    per = 2 * SUB
    steps = count // per
    rows_x, rows_y = whole[4].shape[:2]
    own_blocks = rows_x * rows_y
    window = (rows_x + 2) * (rows_y + 2)
    table = window * blk * latent // 128
    picked = SUB * blk * latent // 128
    return pl.pallas_call(
        edge_kernel,
        grid=(steps,),
        in_specs=[pl.BlockSpec((per, blk, latent), lambda i: (i, 0, 0))]
        + [pl.BlockSpec(memory_space=pltpu.HBM)] * len(whole),
        out_specs=[
            pl.BlockSpec((per, blk, latent), lambda i: (i, 0, 0)),
            pl.BlockSpec((own_blocks, blk, latent), lambda i: (0, 0, 0)),
        ],
        scratch_shapes=[
            pltpu.VMEM((table, 128), jnp.float32),
            pltpu.VMEM((own_blocks, blk, latent), jnp.bfloat16),
            pltpu.VMEM((own_blocks, blk, latent), jnp.float32),
            pltpu.VMEM((picked, 128), jnp.float32),
            pltpu.VMEM((picked, 128), jnp.float32),
        ]
        + [pltpu.SMEM(a.shape, a.dtype) for a in whole[:3]]
        + [pltpu.VMEM(a.shape, a.dtype) for a in whole[3:]]
        + [pltpu.SemaphoreType.DMA((len(whole),))],
        out_shape=[
            jax.ShapeDtypeStruct(edges.shape, edges.dtype),
            jax.ShapeDtypeStruct((own_blocks, blk, latent), jnp.bfloat16),
        ],
        compiler_params=pltpu.CompilerParams(
            vmem_limit_bytes=48 * 2**20, dimension_semantics=("arbitrary",)
        ),
        cost_estimate=pl.CostEstimate(
            flops=20 * 10**9, bytes_accessed=100 * 10**6, transcendentals=5 * 10**6
        ),
        name="edges",
    )(edges, *whole)


def column(row):
    count = row.shape[-1]
    diagonal = lax.broadcasted_iota(jnp.int32, (count, count), 0) == lax.broadcasted_iota(
        jnp.int32, (count, count), 1
    )
    return jnp.sum(jnp.where(diagonal, row, jnp.zeros_like(row)), axis=1, keepdims=True)


def middle_kernel(own, parents, weights, middle, mid_parents, mid_weights, middle_mid, rows_out, *, coarse_own):
    blocks, blk, latent = own.shape
    count = middle.shape[0]
    number = lax.broadcasted_iota(jnp.int32, (count, blk), 0)
    tops = []
    rests = []
    wide = parents.shape[1]
    for b in range(blocks):
        x, y = b // wide, b % wide
        share = jnp.where(parents[x, y : y + 1, :] == number, weights[x, y : y + 1, :], 0.0)
        top = share.astype(jnp.bfloat16)
        tops.append(top)
        rests.append((share - top.astype(jnp.float32)).astype(jnp.bfloat16))
    rows = own[...].reshape(blocks * blk, latent)
    total = matmul(jnp.concatenate(tops, axis=1), rows) + matmul(jnp.concatenate(rests, axis=1), rows)
    mid = (middle[...].astype(jnp.float32) + total).astype(jnp.bfloat16)
    middle_mid[...] = mid
    owner = mid_parents[...] // coarse_own
    place = mid_parents[...] - owner * coarse_own
    devices = rows_out.shape[0]
    mine = owner == lax.broadcasted_iota(jnp.int32, (devices, count), 0)
    rows_out[:, :latent] = matmul(mine.astype(jnp.bfloat16), mid).astype(jnp.bfloat16)
    weight = jnp.sum(jnp.where(mine, mid_weights[...], 0.0), axis=1, keepdims=True)
    spot = jnp.sum(jnp.where(mine, place.astype(jnp.float32), 0.0), axis=1, keepdims=True)
    top = weight.astype(jnp.bfloat16).astype(jnp.float32)
    second = (weight - top).astype(jnp.bfloat16).astype(jnp.float32)
    lane = lax.broadcasted_iota(jnp.int32, (devices, rows_out.shape[1] - latent), 1)
    notes = jnp.where(lane == 0, top, jnp.where(lane == 1, second, jnp.where(lane == 2, weight - top - second, spot)))
    rows_out[:, latent:] = notes.astype(jnp.bfloat16)


def coarse_kernel(rows_in, coarse, first, bias, second, bias_two, gain, result, answers):
    own_count, latent = coarse.shape
    devices = rows_in.shape[0]
    notes = rows_in[:, latent:].astype(jnp.float32)
    lane = lax.broadcasted_iota(jnp.int32, (devices, 128), 1)
    at_place = notes[:, 3:4] == lane.astype(jnp.float32)
    rows = rows_in[:, :latent]
    total = jnp.zeros((128, latent), jnp.float32)
    for n in range(3):
        total += matmul_t(jnp.where(at_place, notes[:, n : n + 1], 0.0).astype(jnp.bfloat16), rows)
    summed = total[:own_count].astype(jnp.bfloat16)
    pre = matmul(coarse[...], first[0]) + matmul(summed, first[1]) + bias[...]
    hidden = silu(pre).astype(jnp.bfloat16)
    out = matmul(hidden, second[...]) + bias_two[...]
    new = coarse[...].astype(jnp.float32) + layer_norm(out, gain[...])
    result[...] = new.astype(jnp.bfloat16)
    padded = jnp.concatenate([new, jnp.zeros((128 - own_count, latent), jnp.float32)], axis=0)
    answers[...] = matmul(at_place.astype(jnp.bfloat16), padded.astype(jnp.bfloat16)).astype(jnp.bfloat16)


def final_kernel(
    own, aggregate, first, bias, second, bias_two, gain,
    middle_mid, from_owners, mid_parents, mid_weights, parents, weights, fine_result, middle_result, *, coarse_own,
):
    blocks, blk, latent = own.shape
    count = middle_mid.shape[0]
    rows = own[...].reshape(blocks * blk, latent)
    pre = matmul(rows, first[0]) + matmul(aggregate[...].reshape(blocks * blk, latent), first[1]) + bias[...]
    out = matmul(silu(pre).astype(jnp.bfloat16), second[...]) + bias_two[...]
    fine_mid = rows.astype(jnp.float32) + layer_norm(out, gain[...])
    devices = from_owners.shape[0]
    mine = mid_parents[...] // coarse_own == lax.broadcasted_iota(jnp.int32, (devices, count), 0)
    from_coarse = matmul_t(mine.astype(jnp.bfloat16), from_owners[...])
    new_middle = (middle_mid[...].astype(jnp.float32) + column(mid_weights[...]) * from_coarse).astype(jnp.bfloat16)
    middle_result[...] = new_middle
    number = lax.broadcasted_iota(jnp.int32, (count, blk), 0)
    wide = parents.shape[1]
    for b in range(blocks):
        x, y = b // wide, b % wide
        from_middle = matmul_t((parents[x, y : y + 1, :] == number).astype(jnp.bfloat16), new_middle)
        fine_result[b] = (
            fine_mid[b * blk : (b + 1) * blk] + column(weights[x, y : y + 1, :]) * from_middle
        ).astype(jnp.bfloat16)


def call(kernel, name, out_shape, *args, **static):
    count = len(args)
    total = count + len(out_shape)

    def run(*refs):
        held = refs[total : total + count]
        bring(refs[:count], held, refs[-1])
        kernel(*held, *refs[count:total], **static)

    return pl.pallas_call(
        run,
        out_shape=out_shape,
        in_specs=[pl.BlockSpec(memory_space=pltpu.HBM)] * count,
        out_specs=[pl.BlockSpec(memory_space=pltpu.VMEM)] * len(out_shape),
        scratch_shapes=[pltpu.VMEM(a.shape, a.dtype) for a in args] + [pltpu.SemaphoreType.DMA((count,))],
        cost_estimate=pl.CostEstimate(flops=10**9, bytes_accessed=9 * 10**6, transcendentals=10**5),
        compiler_params=pltpu.CompilerParams(vmem_limit_bytes=48 * 2**20),
        name=name,
    )(*args)


def exchanged(array, axis, dim):
    count, length = (lax.axis_size(axis), array.shape[dim])
    up = [(i, (i + 1) % count) for i in range(count - 1)]
    down = [(j, i) for i, j in up]
    last = lax.slice_in_dim(array, length - 1, length, axis=dim)
    first = lax.slice_in_dim(array, 0, 1, axis=dim)
    return lax.ppermute(last, axis, up), lax.ppermute(first, axis, down)


def body(
    fine_nodes, edge_states, middle_nodes, coarse_nodes, edge_sources, target_blocks, target_nodes,
    live_blocks, fine_parent, fine_weight, middle_parent, middle_weight,
    edge_in, edge_bias, edge_out, edge_bias_two, edge_gain,
    node_in, node_bias, node_out, node_bias_two, node_gain,
    coarse_in, coarse_bias, coarse_out, coarse_bias_two, coarse_gain,
):
    rows_x, rows_y, blk, latent = fine_nodes.shape
    blocks = rows_x * rows_y
    coarse_own = coarse_nodes.shape[0]
    devices = lax.axis_size(BOTH)
    row = lambda a: a.reshape(1, -1)
    own = fine_nodes.reshape(blocks, blk, latent)
    mid_parents = row(middle_parent)
    mid_weights = row(middle_weight)
    middle = middle_nodes.reshape(-1, latent)
    like = jax.ShapeDtypeStruct

    up, down = exchanged(fine_nodes, "gx", 0)
    middle_mid, rows_out = call(
        middle_kernel, "middle", [like(middle.shape, jnp.bfloat16), like((devices, latent + 128), jnp.bfloat16)],
        own, fine_parent, fine_weight, middle, mid_parents, mid_weights, coarse_own=coarse_own,
    )
    tall = lambda y: jnp.concatenate([up[:, y : y + 1], fine_nodes[:, y : y + 1], down[:, y : y + 1]], axis=0)
    count = lax.axis_size("gy")
    right_pairs = [(i, i + 1) for i in range(count - 1)]
    left = lax.ppermute(tall(rows_y - 1), "gy", right_pairs)
    right = lax.ppermute(tall(0), "gy", [(j, i) for i, j in right_pairs])
    rows_in = lax.all_to_all(rows_out, BOTH, 0, 0, tiled=True)
    edge_result, aggregate = edge_call(
        edge_states[0, 0], edge_sources[0, 0], target_blocks[0], live_blocks, target_nodes[0, 0],
        fine_nodes, up, down, left, right,
        edge_in, row(edge_bias), edge_out, row(edge_bias_two), row(edge_gain),
    )
    coarse_result, answers = call(
        coarse_kernel, "coarse", [like(coarse_nodes.shape, jnp.bfloat16), like((devices, latent), jnp.bfloat16)],
        rows_in, coarse_nodes, coarse_in, row(coarse_bias), coarse_out, row(coarse_bias_two), row(coarse_gain),
    )
    from_owners = lax.all_to_all(answers, BOTH, 0, 0, tiled=True)
    fine_result, middle_result = call(
        final_kernel, "final", [like(own.shape, jnp.bfloat16), like(middle.shape, jnp.bfloat16)],
        own, aggregate, node_in, row(node_bias), node_out, row(node_bias_two), row(node_gain),
        middle_mid, from_owners, mid_parents, mid_weights, fine_parent, fine_weight, coarse_own=coarse_own,
    )
    return (
        fine_result.reshape(fine_nodes.shape),
        edge_result.reshape(edge_states.shape),
        middle_result.reshape(middle_nodes.shape),
        coarse_result,
    )


def solution(mesh):
    placed = (
        P("gx", "gy", None, None),
        P("gx", "gy", None, None, None),
        P("gx", "gy", None, None),
        P(("gx", "gy"), None),
        P("gx", "gy", None, None),
        P("gx", "gy", None),
        P("gx", "gy", None, None),
        P("gx", "gy"),
        P("gx", "gy", None),
        P("gx", "gy", None),
        P("gx", "gy", None),
        P("gx", "gy", None),
        P(),
        P(),
        P(),
        P(),
        P(),
        P(),
        P(),
        P(),
        P(),
        P(),
        P(),
        P(),
        P(),
        P(),
        P(),
    )
    return jax.shard_map(
        body,
        mesh=mesh,
        in_specs=placed,
        out_specs=(
            P("gx", "gy", None, None),
            P("gx", "gy", None, None, None),
            P("gx", "gy", None, None),
            P(("gx", "gy"), None),
        ),
        check_vma=False,
    )
```

```python
import functools
import jax
import jax.numpy as jnp
from jax import lax
from jax.experimental import pallas as pl
from jax.experimental.pallas import tpu as pltpu
from jax.sharding import PartitionSpec as P

epsilon = 1e-05
SUB = 4
BOTH = ("gx", "gy")


def silu(values):
    half = 0.5 * values
    return half * jnp.tanh(half) + half


def layer_norm(values, gain):
    centred = values - jnp.mean(values, axis=-1, keepdims=True)
    spread = jnp.mean(centred * centred, axis=-1, keepdims=True)
    return centred * lax.rsqrt(spread + epsilon) * gain


def matmul(a, b):
    return jnp.dot(a, b, preferred_element_type=jnp.float32)


def matmul_t(a, b):
    return lax.dot_general(a, b, (((0,), (0,)), ((), ())), preferred_element_type=jnp.float32)


WHOLE = 14


def pinned(a):
    return pltpu.with_memory_space_constraint(a, pltpu.HBM)


def bring(whole, held, semaphores):
    copies = [pltpu.make_async_copy(a, b, semaphores.at[n]) for n, (a, b) in enumerate(zip(whole, held))]
    for copy in copies:
        copy.start()
    for copy in copies:
        copy.wait()


def edge_kernel(
    edges, *rest
):
    whole, (result, aggregate, table, targets, sums, picked_a, picked_b), held, semaphores = (
        rest[:WHOLE], rest[WHOLE : WHOLE + 7], rest[WHOLE + 7 : -1], rest[-1]
    )
    (sources, target_blocks, live, target_nodes, own, up, down, left, right, first, bias, second, bias_two, gain) = held
    step = pl.program_id(0)
    steps = pl.num_programs(0)
    picked = (picked_a, picked_b)
    latent = own.shape[-1]
    lanes = 128
    parts = latent // lanes
    blk = 128
    chunks = 2 * steps

    def project(piece, places):
        rows = matmul(piece, first[1]) + bias[...]
        for n, place in enumerate(places):
            for j in range(parts):
                table[pl.ds(place * blk * parts + j, blk, stride=parts), :] = rows[
                    n * blk : (n + 1) * blk, j * lanes : (j + 1) * lanes
                ]

    def gather(chunk, b, into):
        block = chunk * SUB + b
        for e in range(blk):
            at = pl.multiple_of(sources[block, e] * parts, parts)
            into[pl.ds((b * blk + e) * parts, parts), :] = table[pl.ds(at, parts), :]

    @pl.when(step == 0)
    def _():
        bring(whole, held, semaphores)
        rows_x, rows_y = own.shape[0], own.shape[1]
        wide = rows_y + 2
        own_rows = own[...].reshape(-1, latent)
        project(own_rows, [(x + 1) * wide + y + 1 for x in range(rows_x) for y in range(rows_y)])
        project(up[...].reshape(-1, latent), [y + 1 for y in range(rows_y)])
        project(down[...].reshape(-1, latent), [(rows_x + 1) * wide + y + 1 for y in range(rows_y)])
        project(left[...].reshape(-1, latent), [x * wide for x in range(rows_x + 2)])
        project(right[...].reshape(-1, latent), [x * wide + wide - 1 for x in range(rows_x + 2)])
        targets[...] = matmul(own_rows, first[2]).astype(jnp.bfloat16).reshape(targets.shape)
        sums[...] = jnp.zeros_like(sums)
        for b in range(SUB):
            gather(0, b, picked_a)

    number = lax.broadcasted_iota(jnp.int32, (blk, blk), 0)

    def compute(half, b_next):
        chunk = 2 * step + half
        ref = picked[half]
        base = half * SUB
        states = edges[base : base + SUB].reshape(SUB * blk, latent)
        pre = matmul(states, first[0])
        hidden = []
        spots = []
        for b in range(SUB):
            b_next(b)
            block = chunk * SUB + b
            to = target_blocks[0, block]
            spot = (target_nodes[pl.ds(block, 1), :] == number).astype(jnp.bfloat16)
            spots.append((to, spot))
            from_target = matmul_t(spot, targets[to])
            from_source = jnp.concatenate(
                [ref[pl.ds(b * blk * parts + j, blk, stride=parts), :] for j in range(parts)], axis=1
            )
            hidden.append(
                silu(pre[b * blk : (b + 1) * blk] + from_target + from_source).astype(jnp.bfloat16)
            )
        out = matmul(jnp.concatenate(hidden, axis=0), second[...]) + bias_two[...]
        for b in range(SUB):
            rows = out[b * blk : (b + 1) * blk]
            block = chunk * SUB + b
            alive = jnp.where(block < live[0, 0], 1.0, 0.0)
            centred = rows - jnp.mean(rows, axis=-1, keepdims=True)
            spread = jnp.mean(centred * centred, axis=-1, keepdims=True)
            message = (centred * (lax.rsqrt(spread + epsilon) * alive) * gain[...]).astype(jnp.bfloat16)
            result[base + b] = edges[base + b] + message
            to, spot = spots[b]
            sums[to] += matmul(spot, message)

    compute(0, lambda b: gather(2 * step + 1, b, picked_b))
    compute(1, lambda b: gather(jnp.minimum(2 * step + 2, chunks - 1), b, picked_a))

    @pl.when(step == steps - 1)
    def _():
        aggregate[...] = sums[...].astype(aggregate.dtype)


def edge_call(edges, *whole):
    count, blk, latent = edges.shape
    per = 2 * SUB
    steps = count // per
    rows_x, rows_y = whole[4].shape[:2]
    own_blocks = rows_x * rows_y
    window = (rows_x + 2) * (rows_y + 2)
    table = window * blk * latent // 128
    picked = SUB * blk * latent // 128
    return pl.pallas_call(
        edge_kernel,
        grid=(steps,),
        in_specs=[pl.BlockSpec((per, blk, latent), lambda i: (i, 0, 0))]
        + [pl.BlockSpec(memory_space=pltpu.HBM)] * len(whole),
        out_specs=[
            pl.BlockSpec((per, blk, latent), lambda i: (i, 0, 0)),
            pl.BlockSpec((own_blocks, blk, latent), lambda i: (0, 0, 0)),
        ],
        scratch_shapes=[
            pltpu.VMEM((table, 128), jnp.float32),
            pltpu.VMEM((own_blocks, blk, latent), jnp.bfloat16),
            pltpu.VMEM((own_blocks, blk, latent), jnp.float32),
            pltpu.VMEM((picked, 128), jnp.float32),
            pltpu.VMEM((picked, 128), jnp.float32),
        ]
        + [pltpu.SMEM(a.shape, a.dtype) for a in whole[:3]]
        + [pltpu.VMEM(a.shape, a.dtype) for a in whole[3:]]
        + [pltpu.SemaphoreType.DMA((len(whole),))],
        out_shape=[
            jax.ShapeDtypeStruct(edges.shape, edges.dtype),
            jax.ShapeDtypeStruct((own_blocks, blk, latent), jnp.bfloat16),
        ],
        compiler_params=pltpu.CompilerParams(
            vmem_limit_bytes=48 * 2**20, dimension_semantics=("arbitrary",)
        ),
        cost_estimate=pl.CostEstimate(
            flops=20 * 10**9, bytes_accessed=100 * 10**6, transcendentals=5 * 10**6
        ),
        name="edges",
    )(edges, *whole)


def column(row):
    count = row.shape[-1]
    diagonal = lax.broadcasted_iota(jnp.int32, (count, count), 0) == lax.broadcasted_iota(
        jnp.int32, (count, count), 1
    )
    return jnp.sum(jnp.where(diagonal, row, jnp.zeros_like(row)), axis=1, keepdims=True)


def middle_kernel(own, parents, weights, middle, mid_parents, mid_weights, middle_mid, rows_out, *, coarse_own):
    blocks, blk, latent = own.shape
    count = middle.shape[0]
    number = lax.broadcasted_iota(jnp.int32, (count, blk), 0)
    tops = []
    rests = []
    wide = parents.shape[1]
    for b in range(blocks):
        x, y = b // wide, b % wide
        share = jnp.where(parents[x, y : y + 1, :] == number, weights[x, y : y + 1, :], 0.0)
        top = share.astype(jnp.bfloat16)
        tops.append(top)
        rests.append((share - top.astype(jnp.float32)).astype(jnp.bfloat16))
    rows = own[...].reshape(blocks * blk, latent)
    total = matmul(jnp.concatenate(tops, axis=1), rows) + matmul(jnp.concatenate(rests, axis=1), rows)
    mid = (middle[...].astype(jnp.float32) + total).astype(jnp.bfloat16)
    middle_mid[...] = mid
    owner = mid_parents[...] // coarse_own
    place = mid_parents[...] - owner * coarse_own
    devices = rows_out.shape[0]
    mine = owner == lax.broadcasted_iota(jnp.int32, (devices, count), 0)
    rows_mine = matmul(mine.astype(jnp.bfloat16), mid)
    weight = jnp.sum(jnp.where(mine, mid_weights[...], 0.0), axis=1, keepdims=True)
    spot = jnp.sum(jnp.where(mine, place.astype(jnp.float32), 0.0), axis=1, keepdims=True)
    lane = lax.broadcasted_iota(jnp.int32, (devices, 128), 1)
    parts = latent // 128
    for j in range(parts):
        rows_out[:, j, :] = rows_mine[:, j * 128 : (j + 1) * 128]
    rows_out[:, parts, :] = jnp.where(lane == 0, weight, spot)
    for j in range(parts + 1, rows_out.shape[1]):
        rows_out[:, j, :] = jnp.zeros((devices, 128), jnp.float32)


def coarse_kernel(rows_in, coarse, first, bias, second, bias_two, gain, result, answers):
    own_count, latent = coarse.shape
    devices = rows_in.shape[0]
    parts = latent // 128
    weight = rows_in[:, parts, :][:, 0:1]
    spot = rows_in[:, parts, :][:, 1:2]
    lane = lax.broadcasted_iota(jnp.int32, (devices, 128), 1)
    at_place = spot == lane.astype(jnp.float32)
    rows = jnp.concatenate([rows_in[:, j, :] for j in range(parts)], axis=1).astype(jnp.bfloat16)
    total = jnp.zeros((128, latent), jnp.float32)
    for _ in range(3):
        top = weight.astype(jnp.bfloat16).astype(jnp.float32)
        total += matmul_t(jnp.where(at_place, top, 0.0).astype(jnp.bfloat16), rows)
        weight = weight - top
    summed = total[:own_count].astype(jnp.bfloat16)
    pre = matmul(coarse[...], first[0]) + matmul(summed, first[1]) + bias[...]
    hidden = silu(pre).astype(jnp.bfloat16)
    out = matmul(hidden, second[...]) + bias_two[...]
    new = coarse[...].astype(jnp.float32) + layer_norm(out, gain[...])
    result[...] = new.astype(jnp.bfloat16)
    padded = jnp.concatenate([new, jnp.zeros((128 - own_count, latent), jnp.float32)], axis=0)
    answer = matmul(at_place.astype(jnp.bfloat16), padded.astype(jnp.bfloat16))
    for j in range(parts):
        answers[:, j, :] = answer[:, j * 128 : (j + 1) * 128]


def final_kernel(
    own, aggregate, first, bias, second, bias_two, gain,
    middle_mid, from_owners, mid_parents, mid_weights, parents, weights, fine_result, middle_result, *, coarse_own,
):
    blocks, blk, latent = own.shape
    count = middle_mid.shape[0]
    rows = own[...].reshape(blocks * blk, latent)
    pre = matmul(rows, first[0]) + matmul(aggregate[...].reshape(blocks * blk, latent), first[1]) + bias[...]
    out = matmul(silu(pre).astype(jnp.bfloat16), second[...]) + bias_two[...]
    fine_mid = rows.astype(jnp.float32) + layer_norm(out, gain[...])
    devices = from_owners.shape[0]
    mine = mid_parents[...] // coarse_own == lax.broadcasted_iota(jnp.int32, (devices, count), 0)
    answer = jnp.concatenate([from_owners[:, j, :] for j in range(latent // 128)], axis=1)
    from_coarse = matmul_t(mine.astype(jnp.bfloat16), answer.astype(jnp.bfloat16))
    new_middle = (middle_mid[...].astype(jnp.float32) + column(mid_weights[...]) * from_coarse).astype(jnp.bfloat16)
    middle_result[...] = new_middle
    number = lax.broadcasted_iota(jnp.int32, (count, blk), 0)
    wide = parents.shape[1]
    for b in range(blocks):
        x, y = b // wide, b % wide
        from_middle = matmul_t((parents[x, y : y + 1, :] == number).astype(jnp.bfloat16), new_middle)
        fine_result[b] = (
            fine_mid[b * blk : (b + 1) * blk] + column(weights[x, y : y + 1, :]) * from_middle
        ).astype(jnp.bfloat16)


def call(kernel, name, out_shape, *args, **static):
    count = len(args)
    total = count + len(out_shape)

    def run(*refs):
        held = refs[total : total + count]
        bring(refs[:count], held, refs[-1])
        kernel(*held, *refs[count:total], **static)

    return pl.pallas_call(
        run,
        out_shape=out_shape,
        in_specs=[pl.BlockSpec(memory_space=pltpu.HBM)] * count,
        out_specs=[pl.BlockSpec(memory_space=pltpu.VMEM)] * len(out_shape),
        scratch_shapes=[pltpu.VMEM(a.shape, a.dtype) for a in args] + [pltpu.SemaphoreType.DMA((count,))],
        cost_estimate=pl.CostEstimate(flops=10**9, bytes_accessed=9 * 10**6, transcendentals=10**5),
        compiler_params=pltpu.CompilerParams(vmem_limit_bytes=48 * 2**20),
        name=name,
    )(*args)


def exchanged(array, axis, dim):
    count, length = (lax.axis_size(axis), array.shape[dim])
    up = [(i, (i + 1) % count) for i in range(count - 1)]
    down = [(j, i) for i, j in up]
    last = lax.slice_in_dim(array, length - 1, length, axis=dim)
    first = lax.slice_in_dim(array, 0, 1, axis=dim)
    return lax.ppermute(last, axis, up), lax.ppermute(first, axis, down)


def body(
    fine_nodes, edge_states, middle_nodes, coarse_nodes, edge_sources, target_blocks, target_nodes,
    live_blocks, fine_parent, fine_weight, middle_parent, middle_weight,
    edge_in, edge_bias, edge_out, edge_bias_two, edge_gain,
    node_in, node_bias, node_out, node_bias_two, node_gain,
    coarse_in, coarse_bias, coarse_out, coarse_bias_two, coarse_gain,
):
    rows_x, rows_y, blk, latent = fine_nodes.shape
    blocks = rows_x * rows_y
    coarse_own = coarse_nodes.shape[0]
    devices = lax.axis_size(BOTH)
    row = lambda a: a.reshape(1, -1)
    own = fine_nodes.reshape(blocks, blk, latent)
    mid_parents = row(middle_parent)
    mid_weights = row(middle_weight)
    middle = middle_nodes.reshape(-1, latent)
    like = jax.ShapeDtypeStruct

    up, down = exchanged(fine_nodes, "gx", 0)
    middle_mid, rows_out = call(
        middle_kernel, "middle", [like(middle.shape, jnp.bfloat16), like((devices, 8, 128), jnp.float32)],
        *map(pinned, (own, fine_parent, fine_weight, middle, mid_parents, mid_weights)), coarse_own=coarse_own,
    )
    up, down, middle_mid = lax.optimization_barrier((up, down, middle_mid))
    tall = lambda y: jnp.concatenate([up[:, y : y + 1], fine_nodes[:, y : y + 1], down[:, y : y + 1]], axis=0)
    count = lax.axis_size("gy")
    right_pairs = [(i, i + 1) for i in range(count - 1)]
    left = lax.ppermute(tall(rows_y - 1), "gy", right_pairs)
    right = lax.ppermute(tall(0), "gy", [(j, i) for i, j in right_pairs])
    rows_in = lax.all_to_all(rows_out, BOTH, 0, 0, tiled=True)
    coarse_result, answers = call(
        coarse_kernel, "coarse", [like(coarse_nodes.shape, jnp.bfloat16), like((devices, latent // 128, 128), jnp.float32)],
        rows_in,
        *map(pinned, (coarse_nodes, coarse_in, row(coarse_bias), coarse_out, row(coarse_bias_two), row(coarse_gain))),
    )
    live, answers = lax.optimization_barrier((live_blocks, answers))
    edge_result, aggregate = edge_call(
        edge_states[0, 0], pinned(edge_sources[0, 0]), pinned(target_blocks[0]), live, pinned(target_nodes[0, 0]),
        pinned(fine_nodes), up, down, left, right,
        *map(pinned, (edge_in, row(edge_bias), edge_out, row(edge_bias_two), row(edge_gain))),
    )
    from_owners = lax.all_to_all(answers, BOTH, 0, 0, tiled=True)
    fine_result, middle_result = call(
        final_kernel, "final", [like(own.shape, jnp.bfloat16), like(middle.shape, jnp.bfloat16)],
        pinned(own), aggregate,
        *map(pinned, (node_in, row(node_bias), node_out, row(node_bias_two), row(node_gain))),
        middle_mid, from_owners,
        *map(pinned, (mid_parents, mid_weights, fine_parent, fine_weight)), coarse_own=coarse_own,
    )
    return (
        fine_result.reshape(fine_nodes.shape),
        edge_result.reshape(edge_states.shape),
        middle_result.reshape(middle_nodes.shape),
        coarse_result,
    )


def solution(mesh):
    placed = (
        P("gx", "gy", None, None),
        P("gx", "gy", None, None, None),
        P("gx", "gy", None, None),
        P(("gx", "gy"), None),
        P("gx", "gy", None, None),
        P("gx", "gy", None),
        P("gx", "gy", None, None),
        P("gx", "gy"),
        P("gx", "gy", None),
        P("gx", "gy", None),
        P("gx", "gy", None),
        P("gx", "gy", None),
        P(),
        P(),
        P(),
        P(),
        P(),
        P(),
        P(),
        P(),
        P(),
        P(),
        P(),
        P(),
        P(),
        P(),
        P(),
    )
    return jax.shard_map(
        body,
        mesh=mesh,
        in_specs=placed,
        out_specs=(
            P("gx", "gy", None, None),
            P("gx", "gy", None, None, None),
            P("gx", "gy", None, None),
            P(("gx", "gy"), None),
        ),
        check_vma=False,
    )
```

```python
import functools
import jax
import jax.numpy as jnp
from jax import lax
from jax.experimental import pallas as pl
from jax.experimental.pallas import tpu as pltpu
from jax.sharding import PartitionSpec as P

epsilon = 1e-05
SUB = 4
BOTH = ("gx", "gy")


def silu(values):
    half = 0.5 * values
    return half * jnp.tanh(half) + half


def layer_norm(values, gain):
    centred = values - jnp.mean(values, axis=-1, keepdims=True)
    spread = jnp.mean(centred * centred, axis=-1, keepdims=True)
    return centred * lax.rsqrt(spread + epsilon) * gain


def matmul(a, b):
    return jnp.dot(a, b, preferred_element_type=jnp.float32)


def matmul_t(a, b):
    return lax.dot_general(a, b, (((0,), (0,)), ((), ())), preferred_element_type=jnp.float32)


WHOLE = 14


def pinned(a):
    return pltpu.with_memory_space_constraint(a, pltpu.HBM)


def bring(whole, held, semaphores):
    copies = [pltpu.make_async_copy(a, b, semaphores.at[n]) for n, (a, b) in enumerate(zip(whole, held))]
    for copy in copies:
        copy.start()
    for copy in copies:
        copy.wait()


def edge_kernel(
    edges, *rest
):
    whole, (result, aggregate, table, targets, sums, picked_a, picked_b), held, semaphores = (
        rest[:WHOLE], rest[WHOLE : WHOLE + 7], rest[WHOLE + 7 : -1], rest[-1]
    )
    (sources, target_blocks, live, target_nodes, own, up, down, left, right, first, bias, second, bias_two, gain) = held
    step = pl.program_id(0)
    steps = pl.num_programs(0)
    picked = (picked_a, picked_b)
    latent = own.shape[-1]
    lanes = 128
    parts = latent // lanes
    blk = 128
    chunks = 2 * steps

    def project(piece, places):
        rows = matmul(piece, first[1]) + bias[...]
        for n, place in enumerate(places):
            for j in range(parts):
                table[pl.ds(place * blk * parts + j, blk, stride=parts), :] = rows[
                    n * blk : (n + 1) * blk, j * lanes : (j + 1) * lanes
                ]

    def gather(chunk, b, into):
        block = chunk * SUB + b
        for e in range(blk):
            at = pl.multiple_of(sources[block, e] * parts, parts)
            into[pl.ds((b * blk + e) * parts, parts), :] = table[pl.ds(at, parts), :]

    @pl.when(step == 0)
    def _():
        bring(whole, held, semaphores)
        rows_x, rows_y = own.shape[0], own.shape[1]
        wide = rows_y + 2
        own_rows = own[...].reshape(-1, latent)
        project(own_rows, [(x + 1) * wide + y + 1 for x in range(rows_x) for y in range(rows_y)])
        project(up[...].reshape(-1, latent), [y + 1 for y in range(rows_y)])
        project(down[...].reshape(-1, latent), [(rows_x + 1) * wide + y + 1 for y in range(rows_y)])
        project(left[...].reshape(-1, latent), [x * wide for x in range(rows_x + 2)])
        project(right[...].reshape(-1, latent), [x * wide + wide - 1 for x in range(rows_x + 2)])
        targets[...] = matmul(own_rows, first[2]).astype(jnp.bfloat16).reshape(targets.shape)
        sums[...] = jnp.zeros_like(sums)
        for b in range(SUB):
            gather(0, b, picked_a)

    number = lax.broadcasted_iota(jnp.int32, (blk, blk), 0)

    def begin(half, b_next):
        ref = picked[half]
        base = half * SUB
        states = edges[base : base + SUB].reshape(SUB * blk, latent)
        pre = matmul(states, first[0])
        hidden = []
        spots = []
        for b in range(SUB):
            b_next(b)
            block = (2 * step + half) * SUB + b
            to = target_blocks[0, block]
            spot = (target_nodes[pl.ds(block, 1), :] == number).astype(jnp.bfloat16)
            spots.append((to, spot))
            from_target = matmul_t(spot, targets[to])
            from_source = jnp.concatenate(
                [ref[pl.ds(b * blk * parts + j, blk, stride=parts), :] for j in range(parts)], axis=1
            )
            hidden.append(
                silu(pre[b * blk : (b + 1) * blk] + from_target + from_source).astype(jnp.bfloat16)
            )
        return jnp.concatenate(hidden, axis=0), spots

    def finish(half, out, spots):
        base = half * SUB
        for b in range(SUB):
            rows = out[b * blk : (b + 1) * blk]
            block = (2 * step + half) * SUB + b
            alive = jnp.where(block < live[0, 0], 1.0, 0.0)
            centred = rows - jnp.mean(rows, axis=-1, keepdims=True)
            spread = jnp.mean(centred * centred, axis=-1, keepdims=True)
            message = (centred * (lax.rsqrt(spread + epsilon) * alive) * gain[...]).astype(jnp.bfloat16)
            result[base + b] = edges[base + b] + message
            to, spot = spots[b]
            sums[to] += matmul(spot, message)

    hidden_a, spots_a = begin(0, lambda b: gather(2 * step + 1, b, picked_b))
    out_a = matmul(hidden_a, second[...]) + bias_two[...]
    hidden_b, spots_b = begin(1, lambda b: gather(jnp.minimum(2 * step + 2, chunks - 1), b, picked_a))
    out_b = matmul(hidden_b, second[...]) + bias_two[...]
    finish(0, out_a, spots_a)
    finish(1, out_b, spots_b)

    @pl.when(step == steps - 1)
    def _():
        aggregate[...] = sums[...].astype(aggregate.dtype)


def edge_call(edges, *whole):
    count, blk, latent = edges.shape
    per = 2 * SUB
    steps = count // per
    rows_x, rows_y = whole[4].shape[:2]
    own_blocks = rows_x * rows_y
    window = (rows_x + 2) * (rows_y + 2)
    table = window * blk * latent // 128
    picked = SUB * blk * latent // 128
    return pl.pallas_call(
        edge_kernel,
        grid=(steps,),
        in_specs=[pl.BlockSpec((per, blk, latent), lambda i: (i, 0, 0))]
        + [pl.BlockSpec(memory_space=pltpu.HBM)] * len(whole),
        out_specs=[
            pl.BlockSpec((per, blk, latent), lambda i: (i, 0, 0)),
            pl.BlockSpec((own_blocks, blk, latent), lambda i: (0, 0, 0)),
        ],
        scratch_shapes=[
            pltpu.VMEM((table, 128), jnp.float32),
            pltpu.VMEM((own_blocks, blk, latent), jnp.bfloat16),
            pltpu.VMEM((own_blocks, blk, latent), jnp.float32),
            pltpu.VMEM((picked, 128), jnp.float32),
            pltpu.VMEM((picked, 128), jnp.float32),
        ]
        + [pltpu.SMEM(a.shape, a.dtype) for a in whole[:3]]
        + [pltpu.VMEM(a.shape, a.dtype) for a in whole[3:]]
        + [pltpu.SemaphoreType.DMA((len(whole),))],
        out_shape=[
            jax.ShapeDtypeStruct(edges.shape, edges.dtype),
            jax.ShapeDtypeStruct((own_blocks, blk, latent), jnp.bfloat16),
        ],
        compiler_params=pltpu.CompilerParams(
            vmem_limit_bytes=48 * 2**20, dimension_semantics=("arbitrary",)
        ),
        cost_estimate=pl.CostEstimate(
            flops=20 * 10**9, bytes_accessed=100 * 10**6, transcendentals=5 * 10**6
        ),
        name="edges",
    )(edges, *whole)


def column(row):
    count = row.shape[-1]
    diagonal = lax.broadcasted_iota(jnp.int32, (count, count), 0) == lax.broadcasted_iota(
        jnp.int32, (count, count), 1
    )
    return jnp.sum(jnp.where(diagonal, row, jnp.zeros_like(row)), axis=1, keepdims=True)


def middle_kernel(own, parents, weights, middle, mid_parents, mid_weights, middle_mid, rows_out, *, coarse_own):
    blocks, blk, latent = own.shape
    count = middle.shape[0]
    number = lax.broadcasted_iota(jnp.int32, (count, blk), 0)
    tops = []
    rests = []
    wide = parents.shape[1]
    for b in range(blocks):
        x, y = b // wide, b % wide
        share = jnp.where(parents[x, y : y + 1, :] == number, weights[x, y : y + 1, :], 0.0)
        top = share.astype(jnp.bfloat16)
        tops.append(top)
        rests.append((share - top.astype(jnp.float32)).astype(jnp.bfloat16))
    rows = own[...].reshape(blocks * blk, latent)
    total = matmul(jnp.concatenate(tops, axis=1), rows) + matmul(jnp.concatenate(rests, axis=1), rows)
    mid = (middle[...].astype(jnp.float32) + total).astype(jnp.bfloat16)
    middle_mid[...] = mid
    owner = mid_parents[...] // coarse_own
    place = mid_parents[...] - owner * coarse_own
    devices = rows_out.shape[0]
    mine = owner == lax.broadcasted_iota(jnp.int32, (devices, count), 0)
    rows_mine = matmul(mine.astype(jnp.bfloat16), mid)
    weight = jnp.sum(jnp.where(mine, mid_weights[...], 0.0), axis=1, keepdims=True)
    spot = jnp.sum(jnp.where(mine, place.astype(jnp.float32), 0.0), axis=1, keepdims=True)
    lane = lax.broadcasted_iota(jnp.int32, (devices, 128), 1)
    parts = latent // 128
    for j in range(parts):
        rows_out[:, j, :] = rows_mine[:, j * 128 : (j + 1) * 128]
    rows_out[:, parts, :] = jnp.where(lane == 0, weight, spot)
    for j in range(parts + 1, rows_out.shape[1]):
        rows_out[:, j, :] = jnp.zeros((devices, 128), jnp.float32)


def coarse_kernel(rows_in, coarse, first, bias, second, bias_two, gain, result, answers):
    own_count, latent = coarse.shape
    devices = rows_in.shape[0]
    parts = latent // 128
    weight = rows_in[:, parts, :][:, 0:1]
    spot = rows_in[:, parts, :][:, 1:2]
    lane = lax.broadcasted_iota(jnp.int32, (devices, 128), 1)
    at_place = spot == lane.astype(jnp.float32)
    rows = jnp.concatenate([rows_in[:, j, :] for j in range(parts)], axis=1).astype(jnp.bfloat16)
    total = jnp.zeros((128, latent), jnp.float32)
    for _ in range(3):
        top = weight.astype(jnp.bfloat16).astype(jnp.float32)
        total += matmul_t(jnp.where(at_place, top, 0.0).astype(jnp.bfloat16), rows)
        weight = weight - top
    summed = total[:own_count].astype(jnp.bfloat16)
    pre = matmul(coarse[...], first[0]) + matmul(summed, first[1]) + bias[...]
    hidden = silu(pre).astype(jnp.bfloat16)
    out = matmul(hidden, second[...]) + bias_two[...]
    new = coarse[...].astype(jnp.float32) + layer_norm(out, gain[...])
    result[...] = new.astype(jnp.bfloat16)
    padded = jnp.concatenate([new, jnp.zeros((128 - own_count, latent), jnp.float32)], axis=0)
    answer = matmul(at_place.astype(jnp.bfloat16), padded.astype(jnp.bfloat16))
    for j in range(parts):
        answers[:, j, :] = answer[:, j * 128 : (j + 1) * 128]


def node_kernel(own, aggregate, first, bias, second, bias_two, gain, fine_mid):
    blocks, blk, latent = own.shape
    rows = own[...].reshape(blocks * blk, latent)
    pre = matmul(rows, first[0]) + matmul(aggregate[...].reshape(blocks * blk, latent), first[1]) + bias[...]
    out = matmul(silu(pre).astype(jnp.bfloat16), second[...]) + bias_two[...]
    new = rows.astype(jnp.float32) + layer_norm(out, gain[...])
    fine_mid[...] = new.reshape(fine_mid.shape)


def final_kernel(
    fine_mid, middle_mid, from_owners, mid_parents, mid_weights, parents, weights,
    fine_result, middle_result, *, coarse_own,
):
    blocks, blk, latent = fine_mid.shape
    count = middle_mid.shape[0]
    devices = from_owners.shape[0]
    mine = mid_parents[...] // coarse_own == lax.broadcasted_iota(jnp.int32, (devices, count), 0)
    answer = jnp.concatenate([from_owners[:, j, :] for j in range(latent // 128)], axis=1)
    from_coarse = matmul_t(mine.astype(jnp.bfloat16), answer.astype(jnp.bfloat16))
    new_middle = (middle_mid[...].astype(jnp.float32) + column(mid_weights[...]) * from_coarse).astype(jnp.bfloat16)
    middle_result[...] = new_middle
    number = lax.broadcasted_iota(jnp.int32, (count, blk), 0)
    wide = parents.shape[1]
    for b in range(blocks):
        x, y = b // wide, b % wide
        from_middle = matmul_t((parents[x, y : y + 1, :] == number).astype(jnp.bfloat16), new_middle)
        fine_result[b] = (
            fine_mid[b] + column(weights[x, y : y + 1, :]) * from_middle
        ).astype(jnp.bfloat16)


def call(kernel, name, out_shape, *args, **static):
    count = len(args)
    total = count + len(out_shape)

    def run(*refs):
        held = refs[total : total + count]
        bring(refs[:count], held, refs[-1])
        kernel(*held, *refs[count:total], **static)

    return pl.pallas_call(
        run,
        out_shape=out_shape,
        in_specs=[pl.BlockSpec(memory_space=pltpu.HBM)] * count,
        out_specs=[pl.BlockSpec(memory_space=pltpu.VMEM)] * len(out_shape),
        scratch_shapes=[pltpu.VMEM(a.shape, a.dtype) for a in args] + [pltpu.SemaphoreType.DMA((count,))],
        cost_estimate=pl.CostEstimate(flops=10**9, bytes_accessed=9 * 10**6, transcendentals=10**5),
        compiler_params=pltpu.CompilerParams(vmem_limit_bytes=48 * 2**20),
        name=name,
    )(*args)


def exchanged(array, axis, dim):
    count, length = (lax.axis_size(axis), array.shape[dim])
    up = [(i, (i + 1) % count) for i in range(count - 1)]
    down = [(j, i) for i, j in up]
    last = lax.slice_in_dim(array, length - 1, length, axis=dim)
    first = lax.slice_in_dim(array, 0, 1, axis=dim)
    return lax.ppermute(last, axis, up), lax.ppermute(first, axis, down)


def body(
    fine_nodes, edge_states, middle_nodes, coarse_nodes, edge_sources, target_blocks, target_nodes,
    live_blocks, fine_parent, fine_weight, middle_parent, middle_weight,
    edge_in, edge_bias, edge_out, edge_bias_two, edge_gain,
    node_in, node_bias, node_out, node_bias_two, node_gain,
    coarse_in, coarse_bias, coarse_out, coarse_bias_two, coarse_gain,
):
    rows_x, rows_y, blk, latent = fine_nodes.shape
    blocks = rows_x * rows_y
    coarse_own = coarse_nodes.shape[0]
    devices = lax.axis_size(BOTH)
    row = lambda a: a.reshape(1, -1)
    own = fine_nodes.reshape(blocks, blk, latent)
    mid_parents = row(middle_parent)
    mid_weights = row(middle_weight)
    middle = middle_nodes.reshape(-1, latent)
    like = jax.ShapeDtypeStruct

    up, down = exchanged(fine_nodes, "gx", 0)
    middle_mid, rows_out = call(
        middle_kernel, "middle", [like(middle.shape, jnp.bfloat16), like((devices, 8, 128), jnp.float32)],
        *map(pinned, (own, fine_parent, fine_weight, middle, mid_parents, mid_weights)), coarse_own=coarse_own,
    )
    up, down, middle_mid = lax.optimization_barrier((up, down, middle_mid))
    tall = lambda y: jnp.concatenate([up[:, y : y + 1], fine_nodes[:, y : y + 1], down[:, y : y + 1]], axis=0)
    count = lax.axis_size("gy")
    right_pairs = [(i, i + 1) for i in range(count - 1)]
    left = lax.ppermute(tall(rows_y - 1), "gy", right_pairs)
    right = lax.ppermute(tall(0), "gy", [(j, i) for i, j in right_pairs])
    rows_in = lax.all_to_all(rows_out, BOTH, 0, 0, tiled=True)
    edge_result, aggregate = edge_call(
        edge_states[0, 0], pinned(edge_sources[0, 0]), pinned(target_blocks[0]), live_blocks, pinned(target_nodes[0, 0]),
        pinned(fine_nodes), up, down, pinned(left), pinned(right),
        *map(pinned, (edge_in, row(edge_bias), edge_out, row(edge_bias_two), row(edge_gain))),
    )
    rows_in, aggregate = lax.optimization_barrier((rows_in, aggregate))
    coarse_result, answers = call(
        coarse_kernel, "coarse", [like(coarse_nodes.shape, jnp.bfloat16), like((devices, latent // 128, 128), jnp.float32)],
        rows_in,
        *map(pinned, (coarse_nodes, coarse_in, row(coarse_bias), coarse_out, row(coarse_bias_two), row(coarse_gain))),
    )
    from_owners = lax.all_to_all(answers, BOTH, 0, 0, tiled=True)
    (fine_mid,) = call(
        node_kernel, "nodes", [like(own.shape, jnp.float32)],
        pinned(own), aggregate,
        *map(pinned, (node_in, row(node_bias), node_out, row(node_bias_two), row(node_gain))),
    )
    fine_result, middle_result = call(
        final_kernel, "final", [like(own.shape, jnp.bfloat16), like(middle.shape, jnp.bfloat16)],
        fine_mid, middle_mid, from_owners,
        *map(pinned, (mid_parents, mid_weights, fine_parent, fine_weight)), coarse_own=coarse_own,
    )
    return (
        fine_result.reshape(fine_nodes.shape),
        edge_result.reshape(edge_states.shape),
        middle_result.reshape(middle_nodes.shape),
        coarse_result,
    )


def solution(mesh):
    placed = (
        P("gx", "gy", None, None),
        P("gx", "gy", None, None, None),
        P("gx", "gy", None, None),
        P(("gx", "gy"), None),
        P("gx", "gy", None, None),
        P("gx", "gy", None),
        P("gx", "gy", None, None),
        P("gx", "gy"),
        P("gx", "gy", None),
        P("gx", "gy", None),
        P("gx", "gy", None),
        P("gx", "gy", None),
        P(),
        P(),
        P(),
        P(),
        P(),
        P(),
        P(),
        P(),
        P(),
        P(),
        P(),
        P(),
        P(),
        P(),
        P(),
    )
    return jax.shard_map(
        body,
        mesh=mesh,
        in_specs=placed,
        out_specs=(
            P("gx", "gy", None, None),
            P("gx", "gy", None, None, None),
            P("gx", "gy", None, None),
            P(("gx", "gy"), None),
        ),
        check_vma=False,
    )
```

```python
import functools
import jax
import jax.numpy as jnp
from jax import lax
from jax.experimental import pallas as pl
from jax.experimental.pallas import tpu as pltpu
from jax.sharding import PartitionSpec as P

epsilon = 1e-05
SUB = 4
BOTH = ("gx", "gy")


def silu(values):
    half = 0.5 * values
    return half * jnp.tanh(half) + half


def layer_norm(values, gain):
    centred = values - jnp.mean(values, axis=-1, keepdims=True)
    spread = jnp.mean(centred * centred, axis=-1, keepdims=True)
    return centred * lax.rsqrt(spread + epsilon) * gain


def matmul(a, b):
    return jnp.dot(a, b, preferred_element_type=jnp.float32)


def matmul_t(a, b):
    return lax.dot_general(a, b, (((0,), (0,)), ((), ())), preferred_element_type=jnp.float32)


WHOLE = 14


def pinned(a):
    return pltpu.with_memory_space_constraint(a, pltpu.HBM)


def bring(whole, held, semaphores):
    copies = [pltpu.make_async_copy(a, b, semaphores.at[n]) for n, (a, b) in enumerate(zip(whole, held))]
    for copy in copies:
        copy.start()
    for copy in copies:
        copy.wait()


def edge_kernel(
    edges, *rest, start, carried
):
    given = rest[WHOLE : WHOLE + 2] if carried else ()
    rest = rest[:WHOLE] + rest[WHOLE + len(given) :]
    whole, (result, aggregate, table, targets, sums, picked_a, picked_b), held, semaphores = (
        rest[:WHOLE], rest[WHOLE : WHOLE + 7], rest[WHOLE + 7 : -1], rest[-1]
    )
    (sources, target_blocks, live, target_nodes, own, up, down, left, right, first, bias, second, bias_two, gain) = held
    step = pl.program_id(0) + start
    steps = pl.num_programs(0)
    picked = (picked_a, picked_b)
    latent = own.shape[-1]
    lanes = 128
    parts = latent // lanes
    blk = 128
    chunks = 2 * (start + steps)

    def project(piece, places):
        rows = matmul(piece, first[1]) + bias[...]
        for n, place in enumerate(places):
            for j in range(parts):
                table[pl.ds(place * blk * parts + j, blk, stride=parts), :] = rows[
                    n * blk : (n + 1) * blk, j * lanes : (j + 1) * lanes
                ]

    def gather(chunk, b, into):
        block = chunk * SUB + b
        for e in range(blk):
            at = pl.multiple_of(sources[block, e] * parts, parts)
            into[pl.ds((b * blk + e) * parts, parts), :] = table[pl.ds(at, parts), :]

    @pl.when(step == start)
    def _():
        bring(whole, held, semaphores)
        rows_x, rows_y = own.shape[0], own.shape[1]
        wide = rows_y + 2
        own_rows = own[...].reshape(-1, latent)
        project(own_rows, [(x + 1) * wide + y + 1 for x in range(rows_x) for y in range(rows_y)])
        project(up[...].reshape(-1, latent), [y + 1 for y in range(rows_y)])
        project(down[...].reshape(-1, latent), [(rows_x + 1) * wide + y + 1 for y in range(rows_y)])
        project(left[...].reshape(-1, latent), [x * wide for x in range(rows_x + 2)])
        project(right[...].reshape(-1, latent), [x * wide + wide - 1 for x in range(rows_x + 2)])
        targets[...] = matmul(own_rows, first[2]).astype(jnp.bfloat16).reshape(targets.shape)
        if carried:
            pltpu.sync_copy(given[0], sums)
        else:
            sums[...] = jnp.zeros_like(sums)
        for b in range(SUB):
            gather(2 * start, b, picked_a)

    number = lax.broadcasted_iota(jnp.int32, (blk, blk), 0)

    def begin(half, b_next):
        ref = picked[half]
        base = half * SUB
        states = edges[base : base + SUB].reshape(SUB * blk, latent)
        pre = matmul(states, first[0])
        hidden = []
        spots = []
        for b in range(SUB):
            b_next(b)
            block = (2 * step + half) * SUB + b
            to = target_blocks[0, block]
            spot = (target_nodes[pl.ds(block, 1), :] == number).astype(jnp.bfloat16)
            spots.append((to, spot))
            from_target = matmul_t(spot, targets[to])
            from_source = jnp.concatenate(
                [ref[pl.ds(b * blk * parts + j, blk, stride=parts), :] for j in range(parts)], axis=1
            )
            hidden.append(
                silu(pre[b * blk : (b + 1) * blk] + from_target + from_source).astype(jnp.bfloat16)
            )
        return jnp.concatenate(hidden, axis=0), spots

    def finish(half, out, spots):
        base = half * SUB
        for b in range(SUB):
            rows = out[b * blk : (b + 1) * blk]
            block = (2 * step + half) * SUB + b
            alive = jnp.where(block < live[0, 0], 1.0, 0.0)
            centred = rows - jnp.mean(rows, axis=-1, keepdims=True)
            spread = jnp.mean(centred * centred, axis=-1, keepdims=True)
            message = (centred * (lax.rsqrt(spread + epsilon) * alive) * gain[...]).astype(jnp.bfloat16)
            result[base + b] = edges[base + b] + message
            to, spot = spots[b]
            sums[to] += matmul(spot, message)

    hidden_a, spots_a = begin(0, lambda b: gather(2 * step + 1, b, picked_b))
    out_a = matmul(hidden_a, second[...]) + bias_two[...]
    hidden_b, spots_b = begin(1, lambda b: gather(jnp.minimum(2 * step + 2, chunks - 1), b, picked_a))
    out_b = matmul(hidden_b, second[...]) + bias_two[...]
    finish(0, out_a, spots_a)
    finish(1, out_b, spots_b)

    @pl.when(step == start + steps - 1)
    def _():
        aggregate[...] = sums[...].astype(aggregate.dtype)


def edge_call(edges, *whole, start, steps, given=()):
    count, blk, latent = edges.shape
    per = 2 * SUB
    rows_x, rows_y = whole[4].shape[:2]
    own_blocks = rows_x * rows_y
    window = (rows_x + 2) * (rows_y + 2)
    table = window * blk * latent // 128
    picked = SUB * blk * latent // 128
    return pl.pallas_call(
        functools.partial(edge_kernel, start=start, carried=bool(given)),
        grid=(steps,),
        in_specs=[pl.BlockSpec((per, blk, latent), lambda i: (i + start, 0, 0))]
        + [pl.BlockSpec(memory_space=pltpu.HBM)] * (len(whole) + len(given)),
        out_specs=[
            pl.BlockSpec((per, blk, latent), lambda i: (i + start, 0, 0)),
            pl.BlockSpec((own_blocks, blk, latent), lambda i: (0, 0, 0)),
        ],
        scratch_shapes=[
            pltpu.VMEM((table, 128), jnp.float32),
            pltpu.VMEM((own_blocks, blk, latent), jnp.bfloat16),
            pltpu.VMEM((own_blocks, blk, latent), jnp.float32),
            pltpu.VMEM((picked, 128), jnp.float32),
            pltpu.VMEM((picked, 128), jnp.float32),
        ]
        + [pltpu.SMEM(a.shape, a.dtype) for a in whole[:3]]
        + [pltpu.VMEM(a.shape, a.dtype) for a in whole[3:]]
        + [pltpu.SemaphoreType.DMA((len(whole),))],
        out_shape=[
            jax.ShapeDtypeStruct(edges.shape, edges.dtype),
            jax.ShapeDtypeStruct((own_blocks, blk, latent), jnp.bfloat16 if given else jnp.float32),
        ],
        input_output_aliases={len(whole) + 2: 0} if given else {},
        compiler_params=pltpu.CompilerParams(
            vmem_limit_bytes=48 * 2**20, dimension_semantics=("arbitrary",)
        ),
        cost_estimate=pl.CostEstimate(
            flops=steps * 3 * 10**9, bytes_accessed=steps * 14 * 10**6, transcendentals=steps * 10**6
        ),
        name="edges",
    )(edges, *whole, *given)


def column(row):
    count = row.shape[-1]
    diagonal = lax.broadcasted_iota(jnp.int32, (count, count), 0) == lax.broadcasted_iota(
        jnp.int32, (count, count), 1
    )
    return jnp.sum(jnp.where(diagonal, row, jnp.zeros_like(row)), axis=1, keepdims=True)


def middle_kernel(own, parents, weights, middle, mid_parents, mid_weights, middle_mid, rows_out, *, coarse_own):
    blocks, blk, latent = own.shape
    count = middle.shape[0]
    number = lax.broadcasted_iota(jnp.int32, (count, blk), 0)
    tops = []
    rests = []
    wide = parents.shape[1]
    for b in range(blocks):
        x, y = b // wide, b % wide
        share = jnp.where(parents[x, y : y + 1, :] == number, weights[x, y : y + 1, :], 0.0)
        top = share.astype(jnp.bfloat16)
        tops.append(top)
        rests.append((share - top.astype(jnp.float32)).astype(jnp.bfloat16))
    rows = own[...].reshape(blocks * blk, latent)
    total = matmul(jnp.concatenate(tops, axis=1), rows) + matmul(jnp.concatenate(rests, axis=1), rows)
    mid = (middle[...].astype(jnp.float32) + total).astype(jnp.bfloat16)
    middle_mid[...] = mid
    owner = mid_parents[...] // coarse_own
    place = mid_parents[...] - owner * coarse_own
    devices = rows_out.shape[0]
    mine = owner == lax.broadcasted_iota(jnp.int32, (devices, count), 0)
    rows_mine = matmul(mine.astype(jnp.bfloat16), mid)
    weight = jnp.sum(jnp.where(mine, mid_weights[...], 0.0), axis=1, keepdims=True)
    spot = jnp.sum(jnp.where(mine, place.astype(jnp.float32), 0.0), axis=1, keepdims=True)
    lane = lax.broadcasted_iota(jnp.int32, (devices, 128), 1)
    parts = latent // 128
    for j in range(parts):
        rows_out[:, j, :] = rows_mine[:, j * 128 : (j + 1) * 128]
    rows_out[:, parts, :] = jnp.where(lane == 0, weight, spot)
    for j in range(parts + 1, rows_out.shape[1]):
        rows_out[:, j, :] = jnp.zeros((devices, 128), jnp.float32)


def coarse_kernel(rows_in, coarse, first, bias, second, bias_two, gain, result, answers):
    own_count, latent = coarse.shape
    devices = rows_in.shape[0]
    parts = latent // 128
    weight = rows_in[:, parts, :][:, 0:1]
    spot = rows_in[:, parts, :][:, 1:2]
    lane = lax.broadcasted_iota(jnp.int32, (devices, 128), 1)
    at_place = spot == lane.astype(jnp.float32)
    rows = jnp.concatenate([rows_in[:, j, :] for j in range(parts)], axis=1).astype(jnp.bfloat16)
    total = jnp.zeros((128, latent), jnp.float32)
    for _ in range(3):
        top = weight.astype(jnp.bfloat16).astype(jnp.float32)
        total += matmul_t(jnp.where(at_place, top, 0.0).astype(jnp.bfloat16), rows)
        weight = weight - top
    summed = total[:own_count].astype(jnp.bfloat16)
    pre = matmul(coarse[...], first[0]) + matmul(summed, first[1]) + bias[...]
    hidden = silu(pre).astype(jnp.bfloat16)
    out = matmul(hidden, second[...]) + bias_two[...]
    new = coarse[...].astype(jnp.float32) + layer_norm(out, gain[...])
    result[...] = new.astype(jnp.bfloat16)
    padded = jnp.concatenate([new, jnp.zeros((128 - own_count, latent), jnp.float32)], axis=0)
    answer = matmul(at_place.astype(jnp.bfloat16), padded.astype(jnp.bfloat16))
    for j in range(parts):
        answers[:, j, :] = answer[:, j * 128 : (j + 1) * 128]


def final_kernel(
    own, aggregate, first, bias, second, bias_two, gain,
    middle_mid, from_owners, mid_parents, mid_weights, parents, weights, fine_result, middle_result, *, coarse_own,
):
    blocks, blk, latent = own.shape
    count = middle_mid.shape[0]
    rows = own[...].reshape(blocks * blk, latent)
    pre = matmul(rows, first[0]) + matmul(aggregate[...].reshape(blocks * blk, latent), first[1]) + bias[...]
    out = matmul(silu(pre).astype(jnp.bfloat16), second[...]) + bias_two[...]
    fine_mid = rows.astype(jnp.float32) + layer_norm(out, gain[...])
    devices = from_owners.shape[0]
    mine = mid_parents[...] // coarse_own == lax.broadcasted_iota(jnp.int32, (devices, count), 0)
    answer = jnp.concatenate([from_owners[:, j, :] for j in range(latent // 128)], axis=1)
    from_coarse = matmul_t(mine.astype(jnp.bfloat16), answer.astype(jnp.bfloat16))
    new_middle = (middle_mid[...].astype(jnp.float32) + column(mid_weights[...]) * from_coarse).astype(jnp.bfloat16)
    middle_result[...] = new_middle
    number = lax.broadcasted_iota(jnp.int32, (count, blk), 0)
    wide = parents.shape[1]
    for b in range(blocks):
        x, y = b // wide, b % wide
        from_middle = matmul_t((parents[x, y : y + 1, :] == number).astype(jnp.bfloat16), new_middle)
        fine_result[b] = (
            fine_mid[b * blk : (b + 1) * blk] + column(weights[x, y : y + 1, :]) * from_middle
        ).astype(jnp.bfloat16)


def call(kernel, name, out_shape, *args, **static):
    count = len(args)
    total = count + len(out_shape)

    def run(*refs):
        held = refs[total : total + count]
        bring(refs[:count], held, refs[-1])
        kernel(*held, *refs[count:total], **static)

    return pl.pallas_call(
        run,
        out_shape=out_shape,
        in_specs=[pl.BlockSpec(memory_space=pltpu.HBM)] * count,
        out_specs=[pl.BlockSpec(memory_space=pltpu.VMEM)] * len(out_shape),
        scratch_shapes=[pltpu.VMEM(a.shape, a.dtype) for a in args] + [pltpu.SemaphoreType.DMA((count,))],
        cost_estimate=pl.CostEstimate(flops=10**9, bytes_accessed=9 * 10**6, transcendentals=10**5),
        compiler_params=pltpu.CompilerParams(vmem_limit_bytes=48 * 2**20),
        name=name,
    )(*args)


def exchanged(array, axis, dim):
    count, length = (lax.axis_size(axis), array.shape[dim])
    up = [(i, (i + 1) % count) for i in range(count - 1)]
    down = [(j, i) for i, j in up]
    last = lax.slice_in_dim(array, length - 1, length, axis=dim)
    first = lax.slice_in_dim(array, 0, 1, axis=dim)
    return lax.ppermute(last, axis, up), lax.ppermute(first, axis, down)


def body(
    fine_nodes, edge_states, middle_nodes, coarse_nodes, edge_sources, target_blocks, target_nodes,
    live_blocks, fine_parent, fine_weight, middle_parent, middle_weight,
    edge_in, edge_bias, edge_out, edge_bias_two, edge_gain,
    node_in, node_bias, node_out, node_bias_two, node_gain,
    coarse_in, coarse_bias, coarse_out, coarse_bias_two, coarse_gain,
):
    rows_x, rows_y, blk, latent = fine_nodes.shape
    blocks = rows_x * rows_y
    coarse_own = coarse_nodes.shape[0]
    devices = lax.axis_size(BOTH)
    row = lambda a: a.reshape(1, -1)
    own = fine_nodes.reshape(blocks, blk, latent)
    mid_parents = row(middle_parent)
    mid_weights = row(middle_weight)
    middle = middle_nodes.reshape(-1, latent)
    like = jax.ShapeDtypeStruct

    up, down = exchanged(fine_nodes, "gx", 0)
    middle_mid, rows_out = call(
        middle_kernel, "middle", [like(middle.shape, jnp.bfloat16), like((devices, 8, 128), jnp.float32)],
        *map(pinned, (own, fine_parent, fine_weight, middle, mid_parents, mid_weights)), coarse_own=coarse_own,
    )
    up, down, middle_mid = lax.optimization_barrier((up, down, middle_mid))
    tall = lambda y: jnp.concatenate([up[:, y : y + 1], fine_nodes[:, y : y + 1], down[:, y : y + 1]], axis=0)
    count = lax.axis_size("gy")
    right_pairs = [(i, i + 1) for i in range(count - 1)]
    left = lax.ppermute(tall(rows_y - 1), "gy", right_pairs)
    right = lax.ppermute(tall(0), "gy", [(j, i) for i, j in right_pairs])
    rows_in = lax.all_to_all(rows_out, BOTH, 0, 0, tiled=True)
    edge_whole = (
        pinned(target_nodes[0, 0]), pinned(fine_nodes), up, down, pinned(left), pinned(right),
        *map(pinned, (edge_in, row(edge_bias), edge_out, row(edge_bias_two), row(edge_gain))),
    )
    places = (pinned(edge_sources[0, 0]), pinned(target_blocks[0]))
    all_steps = edge_states.shape[2] // (2 * SUB)
    early = all_steps // 4
    partial = edge_call(edge_states[0, 0], *places, live_blocks, *edge_whole, start=0, steps=early)
    early_result, early_sums = partial
    rows_in, early_sums = lax.optimization_barrier((rows_in, early_sums))
    coarse_result, answers = call(
        coarse_kernel, "coarse", [like(coarse_nodes.shape, jnp.bfloat16), like((devices, latent // 128, 128), jnp.float32)],
        rows_in,
        *map(pinned, (coarse_nodes, coarse_in, row(coarse_bias), coarse_out, row(coarse_bias_two), row(coarse_gain))),
    )
    live, answers = lax.optimization_barrier((live_blocks, answers))
    edge_result, aggregate = edge_call(
        edge_states[0, 0], *places, live, *edge_whole, start=early, steps=all_steps - early, given=(pinned(early_sums), early_result)
    )
    from_owners = lax.all_to_all(answers, BOTH, 0, 0, tiled=True)
    fine_result, middle_result = call(
        final_kernel, "final", [like(own.shape, jnp.bfloat16), like(middle.shape, jnp.bfloat16)],
        pinned(own), aggregate,
        *map(pinned, (node_in, row(node_bias), node_out, row(node_bias_two), row(node_gain))),
        middle_mid, from_owners,
        *map(pinned, (mid_parents, mid_weights, fine_parent, fine_weight)), coarse_own=coarse_own,
    )
    return (
        fine_result.reshape(fine_nodes.shape),
        edge_result.reshape(edge_states.shape),
        middle_result.reshape(middle_nodes.shape),
        coarse_result,
    )


def solution(mesh):
    placed = (
        P("gx", "gy", None, None),
        P("gx", "gy", None, None, None),
        P("gx", "gy", None, None),
        P(("gx", "gy"), None),
        P("gx", "gy", None, None),
        P("gx", "gy", None),
        P("gx", "gy", None, None),
        P("gx", "gy"),
        P("gx", "gy", None),
        P("gx", "gy", None),
        P("gx", "gy", None),
        P("gx", "gy", None),
        P(),
        P(),
        P(),
        P(),
        P(),
        P(),
        P(),
        P(),
        P(),
        P(),
        P(),
        P(),
        P(),
        P(),
        P(),
    )
    return jax.shard_map(
        body,
        mesh=mesh,
        in_specs=placed,
        out_specs=(
            P("gx", "gy", None, None),
            P("gx", "gy", None, None, None),
            P("gx", "gy", None, None),
            P(("gx", "gy"), None),
        ),
        check_vma=False,
    )
```

```python
import functools
import jax
import jax.numpy as jnp
from jax import lax
from jax.experimental import pallas as pl
from jax.experimental.pallas import tpu as pltpu
from jax.sharding import PartitionSpec as P

epsilon = 1e-05
SUB = 4
BOTH = ("gx", "gy")


def silu(values):
    half = 0.5 * values
    return half * jnp.tanh(half) + half


def layer_norm(values, gain):
    centred = values - jnp.mean(values, axis=-1, keepdims=True)
    spread = jnp.mean(centred * centred, axis=-1, keepdims=True)
    return centred * lax.rsqrt(spread + epsilon) * gain


def matmul(a, b):
    return jnp.dot(a, b, preferred_element_type=jnp.float32)


def matmul_t(a, b):
    return lax.dot_general(a, b, (((0,), (0,)), ((), ())), preferred_element_type=jnp.float32)


WHOLE = 14


def pinned(a):
    return pltpu.with_memory_space_constraint(a, pltpu.HBM)


def bring(whole, held, semaphores):
    copies = [pltpu.make_async_copy(a, b, semaphores.at[n]) for n, (a, b) in enumerate(zip(whole, held))]
    for copy in copies:
        copy.start()
    for copy in copies:
        copy.wait()


def edge_kernel(
    edges, *rest
):
    whole, (result, aggregate, table, targets, sums, picked_a, picked_b), held, semaphores = (
        rest[:WHOLE], rest[WHOLE : WHOLE + 7], rest[WHOLE + 7 : -1], rest[-1]
    )
    (sources, target_blocks, live, target_nodes, own, up, down, left, right, first, bias, second, bias_two, gain) = held
    step = pl.program_id(0)
    steps = pl.num_programs(0)
    picked = (picked_a, picked_b)
    latent = own.shape[-1]
    lanes = 128
    parts = latent // lanes
    blk = 128
    chunks = 2 * steps

    def project(piece, places):
        rows = matmul(piece, first[1]) + bias[...]
        for n, place in enumerate(places):
            for j in range(parts):
                table[pl.ds(place * blk * parts + j, blk, stride=parts), :] = rows[
                    n * blk : (n + 1) * blk, j * lanes : (j + 1) * lanes
                ]

    def gather(chunk, b, into):
        block = chunk * SUB + b
        for e in range(blk):
            at = pl.multiple_of(sources[block, e] * parts, parts)
            into[pl.ds((b * blk + e) * parts, parts), :] = table[pl.ds(at, parts), :]

    @pl.when(step == 0)
    def _():
        bring(whole, held, semaphores)
        rows_x, rows_y = own.shape[0], own.shape[1]
        wide = rows_y + 2
        own_rows = own[...].reshape(-1, latent)
        project(own_rows, [(x + 1) * wide + y + 1 for x in range(rows_x) for y in range(rows_y)])
        project(up[...].reshape(-1, latent), [y + 1 for y in range(rows_y)])
        project(down[...].reshape(-1, latent), [(rows_x + 1) * wide + y + 1 for y in range(rows_y)])
        project(left[...].reshape(-1, latent), [x * wide for x in range(rows_x + 2)])
        project(right[...].reshape(-1, latent), [x * wide + wide - 1 for x in range(rows_x + 2)])
        targets[...] = matmul(own_rows, first[2]).astype(jnp.bfloat16).reshape(targets.shape)
        sums[...] = jnp.zeros_like(sums)
        for b in range(SUB):
            gather(0, b, picked_a)

    number = lax.broadcasted_iota(jnp.int32, (blk, blk), 0)

    def begin(half, b_next):
        ref = picked[half]
        base = half * SUB
        states = edges[base : base + SUB].reshape(SUB * blk, latent)
        pre = matmul(states, first[0])
        hidden = []
        spots = []
        for b in range(SUB):
            b_next(b)
            block = (2 * step + half) * SUB + b
            to = target_blocks[0, block]
            spot = (target_nodes[pl.ds(block, 1), :] == number).astype(jnp.bfloat16)
            spots.append((to, spot))
            from_target = matmul_t(spot, targets[to])
            from_source = jnp.concatenate(
                [ref[pl.ds(b * blk * parts + j, blk, stride=parts), :] for j in range(parts)], axis=1
            )
            hidden.append(
                silu(pre[b * blk : (b + 1) * blk] + from_target + from_source).astype(jnp.bfloat16)
            )
        return jnp.concatenate(hidden, axis=0), spots

    def finish(half, out, spots):
        base = half * SUB
        for b in range(SUB):
            rows = out[b * blk : (b + 1) * blk]
            block = (2 * step + half) * SUB + b
            alive = jnp.where(block < live[0, 0], 1.0, 0.0)
            centred = rows - jnp.mean(rows, axis=-1, keepdims=True)
            spread = jnp.mean(centred * centred, axis=-1, keepdims=True)
            message = (centred * (lax.rsqrt(spread + epsilon) * alive) * gain[...]).astype(jnp.bfloat16)
            result[base + b] = edges[base + b] + message
            to, spot = spots[b]
            sums[to] += matmul(spot, message)

    hidden_a, spots_a = begin(0, lambda b: gather(2 * step + 1, b, picked_b))
    out_a = matmul(hidden_a, second[...]) + bias_two[...]
    hidden_b, spots_b = begin(1, lambda b: gather(jnp.minimum(2 * step + 2, chunks - 1), b, picked_a))
    out_b = matmul(hidden_b, second[...]) + bias_two[...]
    finish(0, out_a, spots_a)
    finish(1, out_b, spots_b)

    @pl.when(step == steps - 1)
    def _():
        aggregate[...] = sums[...].astype(aggregate.dtype)


def edge_call(edges, *whole):
    count, blk, latent = edges.shape
    per = 2 * SUB
    steps = count // per
    rows_x, rows_y = whole[4].shape[:2]
    own_blocks = rows_x * rows_y
    window = (rows_x + 2) * (rows_y + 2)
    table = window * blk * latent // 128
    picked = SUB * blk * latent // 128
    return pl.pallas_call(
        edge_kernel,
        grid=(steps,),
        in_specs=[pl.BlockSpec((per, blk, latent), lambda i: (i, 0, 0))]
        + [pl.BlockSpec(memory_space=pltpu.HBM)] * len(whole),
        out_specs=[
            pl.BlockSpec((per, blk, latent), lambda i: (i, 0, 0)),
            pl.BlockSpec((own_blocks, blk, latent), lambda i: (0, 0, 0)),
        ],
        scratch_shapes=[
            pltpu.VMEM((table, 128), jnp.float32),
            pltpu.VMEM((own_blocks, blk, latent), jnp.bfloat16),
            pltpu.VMEM((own_blocks, blk, latent), jnp.float32),
            pltpu.VMEM((picked, 128), jnp.float32),
            pltpu.VMEM((picked, 128), jnp.float32),
        ]
        + [pltpu.SMEM(a.shape, a.dtype) for a in whole[:3]]
        + [pltpu.VMEM(a.shape, a.dtype) for a in whole[3:]]
        + [pltpu.SemaphoreType.DMA((len(whole),))],
        out_shape=[
            jax.ShapeDtypeStruct(edges.shape, edges.dtype),
            jax.ShapeDtypeStruct((own_blocks, blk, latent), jnp.bfloat16),
        ],
        compiler_params=pltpu.CompilerParams(
            vmem_limit_bytes=48 * 2**20, dimension_semantics=("arbitrary",)
        ),
        cost_estimate=pl.CostEstimate(
            flops=20 * 10**9, bytes_accessed=100 * 10**6, transcendentals=5 * 10**6
        ),
        name="edges",
    )(edges, *whole)


def column(row):
    count = row.shape[-1]
    diagonal = lax.broadcasted_iota(jnp.int32, (count, count), 0) == lax.broadcasted_iota(
        jnp.int32, (count, count), 1
    )
    return jnp.sum(jnp.where(diagonal, row, jnp.zeros_like(row)), axis=1, keepdims=True)


def middle_kernel(own, parents, weights, middle, mid_parents, mid_weights, middle_mid, rows_out, *, coarse_own):
    blocks, blk, latent = own.shape
    count = middle.shape[0]
    number = lax.broadcasted_iota(jnp.int32, (count, blk), 0)
    tops = []
    rests = []
    wide = parents.shape[1]
    for b in range(blocks):
        x, y = b // wide, b % wide
        share = jnp.where(parents[x, y : y + 1, :] == number, weights[x, y : y + 1, :], 0.0)
        top = share.astype(jnp.bfloat16)
        tops.append(top)
        rests.append((share - top.astype(jnp.float32)).astype(jnp.bfloat16))
    rows = own[...].reshape(blocks * blk, latent)
    total = matmul(jnp.concatenate(tops, axis=1), rows) + matmul(jnp.concatenate(rests, axis=1), rows)
    mid = (middle[...].astype(jnp.float32) + total).astype(jnp.bfloat16)
    middle_mid[...] = mid
    owner = mid_parents[...] // coarse_own
    place = mid_parents[...] - owner * coarse_own
    devices = rows_out.shape[0]
    mine = owner == lax.broadcasted_iota(jnp.int32, (devices, count), 0)
    rows_mine = matmul(mine.astype(jnp.bfloat16), mid)
    weight = jnp.sum(jnp.where(mine, mid_weights[...], 0.0), axis=1, keepdims=True)
    spot = jnp.sum(jnp.where(mine, place.astype(jnp.float32), 0.0), axis=1, keepdims=True)
    lane = lax.broadcasted_iota(jnp.int32, (devices, 128), 1)
    parts = latent // 128
    for j in range(parts):
        rows_out[:, j, :] = rows_mine[:, j * 128 : (j + 1) * 128]
    rows_out[:, parts, :] = jnp.where(lane == 0, weight, spot)
    for j in range(parts + 1, rows_out.shape[1]):
        rows_out[:, j, :] = jnp.zeros((devices, 128), jnp.float32)


def coarse_kernel(rows_in, coarse, first, bias, second, bias_two, gain, result, answers):
    own_count, latent = coarse.shape
    devices = rows_in.shape[0]
    parts = latent // 128
    weight = rows_in[:, parts, :][:, 0:1]
    spot = rows_in[:, parts, :][:, 1:2]
    lane = lax.broadcasted_iota(jnp.int32, (devices, 128), 1)
    at_place = spot == lane.astype(jnp.float32)
    rows = jnp.concatenate([rows_in[:, j, :] for j in range(parts)], axis=1).astype(jnp.bfloat16)
    total = jnp.zeros((128, latent), jnp.float32)
    for _ in range(3):
        top = weight.astype(jnp.bfloat16).astype(jnp.float32)
        total += matmul_t(jnp.where(at_place, top, 0.0).astype(jnp.bfloat16), rows)
        weight = weight - top
    summed = total[:own_count].astype(jnp.bfloat16)
    pre = matmul(coarse[...], first[0]) + matmul(summed, first[1]) + bias[...]
    hidden = silu(pre).astype(jnp.bfloat16)
    out = matmul(hidden, second[...]) + bias_two[...]
    new = coarse[...].astype(jnp.float32) + layer_norm(out, gain[...])
    result[...] = new.astype(jnp.bfloat16)
    padded = jnp.concatenate([new, jnp.zeros((128 - own_count, latent), jnp.float32)], axis=0)
    answer = matmul(at_place.astype(jnp.bfloat16), padded.astype(jnp.bfloat16))
    for j in range(parts):
        answers[:, j, :] = answer[:, j * 128 : (j + 1) * 128]


def final_kernel(
    own, aggregate, first, bias, second, bias_two, gain,
    middle_mid, from_owners, mid_parents, mid_weights, parents, weights, fine_result, middle_result, *, coarse_own,
):
    blocks, blk, latent = own.shape
    count = middle_mid.shape[0]
    rows = own[...].reshape(blocks * blk, latent)
    pre = matmul(rows, first[0]) + matmul(aggregate[...].reshape(blocks * blk, latent), first[1]) + bias[...]
    out = matmul(silu(pre).astype(jnp.bfloat16), second[...]) + bias_two[...]
    fine_mid = rows.astype(jnp.float32) + layer_norm(out, gain[...])
    devices = from_owners.shape[0]
    mine = mid_parents[...] // coarse_own == lax.broadcasted_iota(jnp.int32, (devices, count), 0)
    answer = jnp.concatenate([from_owners[:, j, :] for j in range(latent // 128)], axis=1)
    from_coarse = matmul_t(mine.astype(jnp.bfloat16), answer.astype(jnp.bfloat16))
    new_middle = (middle_mid[...].astype(jnp.float32) + column(mid_weights[...]) * from_coarse).astype(jnp.bfloat16)
    middle_result[...] = new_middle
    number = lax.broadcasted_iota(jnp.int32, (count, blk), 0)
    wide = parents.shape[1]
    for b in range(blocks):
        x, y = b // wide, b % wide
        from_middle = matmul_t((parents[x, y : y + 1, :] == number).astype(jnp.bfloat16), new_middle)
        fine_result[b] = (
            fine_mid[b * blk : (b + 1) * blk] + column(weights[x, y : y + 1, :]) * from_middle
        ).astype(jnp.bfloat16)


def call(kernel, name, out_shape, *args, **static):
    count = len(args)
    total = count + len(out_shape)

    def run(*refs):
        held = refs[total : total + count]
        bring(refs[:count], held, refs[-1])
        kernel(*held, *refs[count:total], **static)

    return pl.pallas_call(
        run,
        out_shape=out_shape,
        in_specs=[pl.BlockSpec(memory_space=pltpu.HBM)] * count,
        out_specs=[pl.BlockSpec(memory_space=pltpu.VMEM)] * len(out_shape),
        scratch_shapes=[pltpu.VMEM(a.shape, a.dtype) for a in args] + [pltpu.SemaphoreType.DMA((count,))],
        cost_estimate=pl.CostEstimate(flops=10**9, bytes_accessed=9 * 10**6, transcendentals=10**5),
        compiler_params=pltpu.CompilerParams(vmem_limit_bytes=48 * 2**20),
        name=name,
    )(*args)


def exchanged(array, axis, dim):
    count, length = (lax.axis_size(axis), array.shape[dim])
    up = [(i, (i + 1) % count) for i in range(count - 1)]
    down = [(j, i) for i, j in up]
    last = lax.slice_in_dim(array, length - 1, length, axis=dim)
    first = lax.slice_in_dim(array, 0, 1, axis=dim)
    return lax.ppermute(last, axis, up), lax.ppermute(first, axis, down)


def body(
    fine_nodes, edge_states, middle_nodes, coarse_nodes, edge_sources, target_blocks, target_nodes,
    live_blocks, fine_parent, fine_weight, middle_parent, middle_weight,
    edge_in, edge_bias, edge_out, edge_bias_two, edge_gain,
    node_in, node_bias, node_out, node_bias_two, node_gain,
    coarse_in, coarse_bias, coarse_out, coarse_bias_two, coarse_gain,
):
    rows_x, rows_y, blk, latent = fine_nodes.shape
    blocks = rows_x * rows_y
    coarse_own = coarse_nodes.shape[0]
    devices = lax.axis_size(BOTH)
    row = lambda a: a.reshape(1, -1)
    own = fine_nodes.reshape(blocks, blk, latent)
    mid_parents = row(middle_parent)
    mid_weights = row(middle_weight)
    middle = middle_nodes.reshape(-1, latent)
    like = jax.ShapeDtypeStruct

    up, down = exchanged(fine_nodes, "gx", 0)
    middle_mid, rows_out = call(
        middle_kernel, "middle", [like(middle.shape, jnp.bfloat16), like((devices, 8, 128), jnp.float32)],
        *map(pinned, (own, fine_parent, fine_weight, middle, mid_parents, mid_weights)), coarse_own=coarse_own,
    )
    rows_in = lax.all_to_all(rows_out, BOTH, 0, 0, tiled=True)
    up, down, rows_in = lax.optimization_barrier((up, down, rows_in))
    tall = lambda y: jnp.concatenate([up[:, y : y + 1], fine_nodes[:, y : y + 1], down[:, y : y + 1]], axis=0)
    count = lax.axis_size("gy")
    right_pairs = [(i, i + 1) for i in range(count - 1)]
    left = lax.ppermute(tall(rows_y - 1), "gy", right_pairs)
    right = lax.ppermute(tall(0), "gy", [(j, i) for i, j in right_pairs])
    coarse_result, answers = call(
        coarse_kernel, "coarse", [like(coarse_nodes.shape, jnp.bfloat16), like((devices, latent // 128, 128), jnp.float32)],
        rows_in,
        *map(pinned, (coarse_nodes, coarse_in, row(coarse_bias), coarse_out, row(coarse_bias_two), row(coarse_gain))),
    )
    live, answers = lax.optimization_barrier((live_blocks, answers))
    edge_result, aggregate = edge_call(
        edge_states[0, 0], pinned(edge_sources[0, 0]), pinned(target_blocks[0]), live, pinned(target_nodes[0, 0]),
        pinned(fine_nodes), up, down, left, right,
        *map(pinned, (edge_in, row(edge_bias), edge_out, row(edge_bias_two), row(edge_gain))),
    )
    from_owners = lax.all_to_all(answers, BOTH, 0, 0, tiled=True)
    fine_result, middle_result = call(
        final_kernel, "final", [like(own.shape, jnp.bfloat16), like(middle.shape, jnp.bfloat16)],
        pinned(own), aggregate,
        *map(pinned, (node_in, row(node_bias), node_out, row(node_bias_two), row(node_gain))),
        middle_mid, from_owners,
        *map(pinned, (mid_parents, mid_weights, fine_parent, fine_weight)), coarse_own=coarse_own,
    )
    return (
        fine_result.reshape(fine_nodes.shape),
        edge_result.reshape(edge_states.shape),
        middle_result.reshape(middle_nodes.shape),
        coarse_result,
    )


def solution(mesh):
    placed = (
        P("gx", "gy", None, None),
        P("gx", "gy", None, None, None),
        P("gx", "gy", None, None),
        P(("gx", "gy"), None),
        P("gx", "gy", None, None),
        P("gx", "gy", None),
        P("gx", "gy", None, None),
        P("gx", "gy"),
        P("gx", "gy", None),
        P("gx", "gy", None),
        P("gx", "gy", None),
        P("gx", "gy", None),
        P(),
        P(),
        P(),
        P(),
        P(),
        P(),
        P(),
        P(),
        P(),
        P(),
        P(),
        P(),
        P(),
        P(),
        P(),
    )
    return jax.shard_map(
        body,
        mesh=mesh,
        in_specs=placed,
        out_specs=(
            P("gx", "gy", None, None),
            P("gx", "gy", None, None, None),
            P("gx", "gy", None, None),
            P(("gx", "gy"), None),
        ),
        check_vma=False,
    )
```

```python
import functools
import jax
import jax.numpy as jnp
from jax import lax
from jax.experimental import pallas as pl
from jax.experimental.pallas import tpu as pltpu
from jax.sharding import PartitionSpec as P

epsilon = 1e-05
SUB = 4
BOTH = ("gx", "gy")


def silu(values):
    half = 0.5 * values
    return half * jnp.tanh(half) + half


def layer_norm(values, gain):
    centred = values - jnp.mean(values, axis=-1, keepdims=True)
    spread = jnp.mean(centred * centred, axis=-1, keepdims=True)
    return centred * lax.rsqrt(spread + epsilon) * gain


def matmul(a, b):
    return jnp.dot(a, b, preferred_element_type=jnp.float32)


def matmul_t(a, b):
    return lax.dot_general(a, b, (((0,), (0,)), ((), ())), preferred_element_type=jnp.float32)


WHOLE = 14


def pinned(a):
    return pltpu.with_memory_space_constraint(a, pltpu.HBM)


def bring(whole, held, semaphores):
    copies = [pltpu.make_async_copy(a, b, semaphores.at[n]) for n, (a, b) in enumerate(zip(whole, held))]
    for copy in copies:
        copy.start()
    for copy in copies:
        copy.wait()


def edge_kernel(
    edges, *rest
):
    whole, (result, aggregate, table, targets, sums, picked_a, picked_b), held, semaphores = (
        rest[:WHOLE], rest[WHOLE : WHOLE + 7], rest[WHOLE + 7 : -1], rest[-1]
    )
    (sources, target_blocks, live, target_nodes, own, up, down, left, right, first, bias, second, bias_two, gain) = held
    step = pl.program_id(0)
    steps = pl.num_programs(0)
    picked = (picked_a, picked_b)
    latent = own.shape[-1]
    lanes = 128
    parts = latent // lanes
    blk = 128
    chunks = 2 * steps

    def project(piece, places):
        rows = matmul(piece, first[1]) + bias[...]
        for n, place in enumerate(places):
            for j in range(parts):
                table[pl.ds(place * blk * parts + j, blk, stride=parts), :] = rows[
                    n * blk : (n + 1) * blk, j * lanes : (j + 1) * lanes
                ]

    def gather(chunk, b, into):
        block = chunk * SUB + b
        for e in range(blk):
            at = pl.multiple_of(sources[block, e] * parts, parts)
            into[pl.ds((b * blk + e) * parts, parts), :] = table[pl.ds(at, parts), :]

    @pl.when(step == 0)
    def _():
        copies = [pltpu.make_async_copy(a, b, semaphores.at[n]) for n, (a, b) in enumerate(zip(whole, held))]
        soon, sides = (4, 9, 10), (5, 6, 7, 8)
        later = tuple(n for n in range(len(copies)) if n not in soon + sides)
        for n in soon + sides + later:
            copies[n].start()
        for n in soon:
            copies[n].wait()
        rows_x, rows_y = own.shape[0], own.shape[1]
        wide = rows_y + 2
        own_rows = own[...].reshape(-1, latent)
        project(own_rows, [(x + 1) * wide + y + 1 for x in range(rows_x) for y in range(rows_y)])
        targets[...] = matmul(own_rows, first[2]).astype(jnp.bfloat16).reshape(targets.shape)
        sums[...] = jnp.zeros_like(sums)
        for n in sides:
            copies[n].wait()
        project(up[...].reshape(-1, latent), [y + 1 for y in range(rows_y)])
        project(down[...].reshape(-1, latent), [(rows_x + 1) * wide + y + 1 for y in range(rows_y)])
        project(left[...].reshape(-1, latent), [x * wide for x in range(rows_x + 2)])
        project(right[...].reshape(-1, latent), [x * wide + wide - 1 for x in range(rows_x + 2)])
        for n in later:
            copies[n].wait()
        for b in range(SUB):
            gather(0, b, picked_a)

    number = lax.broadcasted_iota(jnp.int32, (blk, blk), 0)

    def begin(half, b_next):
        ref = picked[half]
        base = half * SUB
        states = edges[base : base + SUB].reshape(SUB * blk, latent)
        pre = matmul(states, first[0])
        hidden = []
        spots = []
        for b in range(SUB):
            b_next(b)
            block = (2 * step + half) * SUB + b
            to = target_blocks[0, block]
            spot = (target_nodes[pl.ds(block, 1), :] == number).astype(jnp.bfloat16)
            spots.append((to, spot))
            from_target = matmul_t(spot, targets[to])
            from_source = jnp.concatenate(
                [ref[pl.ds(b * blk * parts + j, blk, stride=parts), :] for j in range(parts)], axis=1
            )
            hidden.append(
                silu(pre[b * blk : (b + 1) * blk] + from_target + from_source).astype(jnp.bfloat16)
            )
        return jnp.concatenate(hidden, axis=0), spots

    def finish(half, out, spots):
        base = half * SUB
        for b in range(SUB):
            rows = out[b * blk : (b + 1) * blk]
            block = (2 * step + half) * SUB + b
            alive = jnp.where(block < live[0, 0], 1.0, 0.0)
            centred = rows - jnp.mean(rows, axis=-1, keepdims=True)
            spread = jnp.mean(centred * centred, axis=-1, keepdims=True)
            message = (centred * (lax.rsqrt(spread + epsilon) * alive) * gain[...]).astype(jnp.bfloat16)
            result[base + b] = edges[base + b] + message
            to, spot = spots[b]
            sums[to] += matmul(spot, message)

    hidden_a, spots_a = begin(0, lambda b: gather(2 * step + 1, b, picked_b))
    out_a = matmul(hidden_a, second[...]) + bias_two[...]
    hidden_b, spots_b = begin(1, lambda b: gather(jnp.minimum(2 * step + 2, chunks - 1), b, picked_a))
    out_b = matmul(hidden_b, second[...]) + bias_two[...]
    finish(0, out_a, spots_a)
    finish(1, out_b, spots_b)

    @pl.when(step == steps - 1)
    def _():
        aggregate[...] = sums[...].astype(aggregate.dtype)


def edge_call(edges, *whole):
    count, blk, latent = edges.shape
    per = 2 * SUB
    steps = count // per
    rows_x, rows_y = whole[4].shape[:2]
    own_blocks = rows_x * rows_y
    window = (rows_x + 2) * (rows_y + 2)
    table = window * blk * latent // 128
    picked = SUB * blk * latent // 128
    return pl.pallas_call(
        edge_kernel,
        grid=(steps,),
        in_specs=[pl.BlockSpec((per, blk, latent), lambda i: (i, 0, 0))]
        + [pl.BlockSpec(memory_space=pltpu.HBM)] * len(whole),
        out_specs=[
            pl.BlockSpec((per, blk, latent), lambda i: (i, 0, 0)),
            pl.BlockSpec((own_blocks, blk, latent), lambda i: (0, 0, 0)),
        ],
        scratch_shapes=[
            pltpu.VMEM((table, 128), jnp.float32),
            pltpu.VMEM((own_blocks, blk, latent), jnp.bfloat16),
            pltpu.VMEM((own_blocks, blk, latent), jnp.float32),
            pltpu.VMEM((picked, 128), jnp.float32),
            pltpu.VMEM((picked, 128), jnp.float32),
        ]
        + [pltpu.SMEM(a.shape, a.dtype) for a in whole[:3]]
        + [pltpu.VMEM(a.shape, a.dtype) for a in whole[3:]]
        + [pltpu.SemaphoreType.DMA((len(whole),))],
        out_shape=[
            jax.ShapeDtypeStruct(edges.shape, edges.dtype),
            jax.ShapeDtypeStruct((own_blocks, blk, latent), jnp.bfloat16),
        ],
        compiler_params=pltpu.CompilerParams(
            vmem_limit_bytes=48 * 2**20, dimension_semantics=("arbitrary",)
        ),
        cost_estimate=pl.CostEstimate(
            flops=20 * 10**9, bytes_accessed=100 * 10**6, transcendentals=5 * 10**6
        ),
        name="edges",
    )(edges, *whole)


def column(row):
    count = row.shape[-1]
    diagonal = lax.broadcasted_iota(jnp.int32, (count, count), 0) == lax.broadcasted_iota(
        jnp.int32, (count, count), 1
    )
    return jnp.sum(jnp.where(diagonal, row, jnp.zeros_like(row)), axis=1, keepdims=True)


def middle_kernel(own, parents, weights, middle, mid_parents, mid_weights, middle_mid, rows_out, *, coarse_own):
    blocks, blk, latent = own.shape
    count = middle.shape[0]
    number = lax.broadcasted_iota(jnp.int32, (count, blk), 0)
    tops = []
    rests = []
    wide = parents.shape[1]
    for b in range(blocks):
        x, y = b // wide, b % wide
        share = jnp.where(parents[x, y : y + 1, :] == number, weights[x, y : y + 1, :], 0.0)
        top = share.astype(jnp.bfloat16)
        tops.append(top)
        rests.append((share - top.astype(jnp.float32)).astype(jnp.bfloat16))
    rows = own[...].reshape(blocks * blk, latent)
    total = matmul(jnp.concatenate(tops, axis=1), rows) + matmul(jnp.concatenate(rests, axis=1), rows)
    mid = (middle[...].astype(jnp.float32) + total).astype(jnp.bfloat16)
    middle_mid[...] = mid
    owner = mid_parents[...] // coarse_own
    place = mid_parents[...] - owner * coarse_own
    devices = rows_out.shape[0]
    mine = owner == lax.broadcasted_iota(jnp.int32, (devices, count), 0)
    rows_mine = matmul(mine.astype(jnp.bfloat16), mid)
    weight = jnp.sum(jnp.where(mine, mid_weights[...], 0.0), axis=1, keepdims=True)
    spot = jnp.sum(jnp.where(mine, place.astype(jnp.float32), 0.0), axis=1, keepdims=True)
    lane = lax.broadcasted_iota(jnp.int32, (devices, 128), 1)
    parts = latent // 128
    for j in range(parts):
        rows_out[:, j, :] = rows_mine[:, j * 128 : (j + 1) * 128]
    rows_out[:, parts, :] = jnp.where(lane == 0, weight, spot)
    for j in range(parts + 1, rows_out.shape[1]):
        rows_out[:, j, :] = jnp.zeros((devices, 128), jnp.float32)


def coarse_kernel(rows_in, coarse, first, bias, second, bias_two, gain, result, answers):
    own_count, latent = coarse.shape
    devices = rows_in.shape[0]
    parts = latent // 128
    weight = rows_in[:, parts, :][:, 0:1]
    spot = rows_in[:, parts, :][:, 1:2]
    lane = lax.broadcasted_iota(jnp.int32, (devices, 128), 1)
    at_place = spot == lane.astype(jnp.float32)
    rows = jnp.concatenate([rows_in[:, j, :] for j in range(parts)], axis=1).astype(jnp.bfloat16)
    total = jnp.zeros((128, latent), jnp.float32)
    for _ in range(3):
        top = weight.astype(jnp.bfloat16).astype(jnp.float32)
        total += matmul_t(jnp.where(at_place, top, 0.0).astype(jnp.bfloat16), rows)
        weight = weight - top
    summed = total[:own_count].astype(jnp.bfloat16)
    pre = matmul(coarse[...], first[0]) + matmul(summed, first[1]) + bias[...]
    hidden = silu(pre).astype(jnp.bfloat16)
    out = matmul(hidden, second[...]) + bias_two[...]
    new = coarse[...].astype(jnp.float32) + layer_norm(out, gain[...])
    result[...] = new.astype(jnp.bfloat16)
    padded = jnp.concatenate([new, jnp.zeros((128 - own_count, latent), jnp.float32)], axis=0)
    answer = matmul(at_place.astype(jnp.bfloat16), padded.astype(jnp.bfloat16))
    for j in range(parts):
        answers[:, j, :] = answer[:, j * 128 : (j + 1) * 128]


def final_kernel(
    own, aggregate, first, bias, second, bias_two, gain,
    middle_mid, from_owners, mid_parents, mid_weights, parents, weights, fine_result, middle_result, *, coarse_own,
):
    blocks, blk, latent = own.shape
    count = middle_mid.shape[0]
    rows = own[...].reshape(blocks * blk, latent)
    pre = matmul(rows, first[0]) + matmul(aggregate[...].reshape(blocks * blk, latent), first[1]) + bias[...]
    out = matmul(silu(pre).astype(jnp.bfloat16), second[...]) + bias_two[...]
    fine_mid = rows.astype(jnp.float32) + layer_norm(out, gain[...])
    devices = from_owners.shape[0]
    mine = mid_parents[...] // coarse_own == lax.broadcasted_iota(jnp.int32, (devices, count), 0)
    answer = jnp.concatenate([from_owners[:, j, :] for j in range(latent // 128)], axis=1)
    from_coarse = matmul_t(mine.astype(jnp.bfloat16), answer.astype(jnp.bfloat16))
    new_middle = (middle_mid[...].astype(jnp.float32) + column(mid_weights[...]) * from_coarse).astype(jnp.bfloat16)
    middle_result[...] = new_middle
    number = lax.broadcasted_iota(jnp.int32, (count, blk), 0)
    wide = parents.shape[1]
    for b in range(blocks):
        x, y = b // wide, b % wide
        from_middle = matmul_t((parents[x, y : y + 1, :] == number).astype(jnp.bfloat16), new_middle)
        fine_result[b] = (
            fine_mid[b * blk : (b + 1) * blk] + column(weights[x, y : y + 1, :]) * from_middle
        ).astype(jnp.bfloat16)


def call(kernel, name, out_shape, *args, **static):
    count = len(args)
    total = count + len(out_shape)

    def run(*refs):
        held = refs[total : total + count]
        bring(refs[:count], held, refs[-1])
        kernel(*held, *refs[count:total], **static)

    return pl.pallas_call(
        run,
        out_shape=out_shape,
        in_specs=[pl.BlockSpec(memory_space=pltpu.HBM)] * count,
        out_specs=[pl.BlockSpec(memory_space=pltpu.VMEM)] * len(out_shape),
        scratch_shapes=[pltpu.VMEM(a.shape, a.dtype) for a in args] + [pltpu.SemaphoreType.DMA((count,))],
        cost_estimate=pl.CostEstimate(flops=10**9, bytes_accessed=9 * 10**6, transcendentals=10**5),
        compiler_params=pltpu.CompilerParams(vmem_limit_bytes=48 * 2**20),
        name=name,
    )(*args)


def exchanged(array, axis, dim):
    count, length = (lax.axis_size(axis), array.shape[dim])
    up = [(i, (i + 1) % count) for i in range(count - 1)]
    down = [(j, i) for i, j in up]
    last = lax.slice_in_dim(array, length - 1, length, axis=dim)
    first = lax.slice_in_dim(array, 0, 1, axis=dim)
    return lax.ppermute(last, axis, up), lax.ppermute(first, axis, down)


def body(
    fine_nodes, edge_states, middle_nodes, coarse_nodes, edge_sources, target_blocks, target_nodes,
    live_blocks, fine_parent, fine_weight, middle_parent, middle_weight,
    edge_in, edge_bias, edge_out, edge_bias_two, edge_gain,
    node_in, node_bias, node_out, node_bias_two, node_gain,
    coarse_in, coarse_bias, coarse_out, coarse_bias_two, coarse_gain,
):
    rows_x, rows_y, blk, latent = fine_nodes.shape
    blocks = rows_x * rows_y
    coarse_own = coarse_nodes.shape[0]
    devices = lax.axis_size(BOTH)
    row = lambda a: a.reshape(1, -1)
    own = fine_nodes.reshape(blocks, blk, latent)
    mid_parents = row(middle_parent)
    mid_weights = row(middle_weight)
    middle = middle_nodes.reshape(-1, latent)
    like = jax.ShapeDtypeStruct

    up, down = exchanged(fine_nodes, "gx", 0)
    middle_mid, rows_out = call(
        middle_kernel, "middle", [like(middle.shape, jnp.bfloat16), like((devices, 8, 128), jnp.float32)],
        *map(pinned, (own, fine_parent, fine_weight, middle, mid_parents, mid_weights)), coarse_own=coarse_own,
    )
    rows_in = lax.all_to_all(rows_out, BOTH, 0, 0, tiled=True)
    up, down, rows_in = lax.optimization_barrier((up, down, rows_in))
    tall = lambda y: jnp.concatenate([up[:, y : y + 1], fine_nodes[:, y : y + 1], down[:, y : y + 1]], axis=0)
    count = lax.axis_size("gy")
    right_pairs = [(i, i + 1) for i in range(count - 1)]
    left = lax.ppermute(tall(rows_y - 1), "gy", right_pairs)
    right = lax.ppermute(tall(0), "gy", [(j, i) for i, j in right_pairs])
    coarse_result, answers = call(
        coarse_kernel, "coarse", [like(coarse_nodes.shape, jnp.bfloat16), like((devices, latent // 128, 128), jnp.float32)],
        rows_in,
        *map(pinned, (coarse_nodes, coarse_in, row(coarse_bias), coarse_out, row(coarse_bias_two), row(coarse_gain))),
    )
    live, answers = lax.optimization_barrier((live_blocks, answers))
    edge_result, aggregate = edge_call(
        edge_states[0, 0], pinned(edge_sources[0, 0]), pinned(target_blocks[0]), live, pinned(target_nodes[0, 0]),
        pinned(fine_nodes), up, down, left, right,
        *map(pinned, (edge_in, row(edge_bias), edge_out, row(edge_bias_two), row(edge_gain))),
    )
    from_owners = lax.all_to_all(answers, BOTH, 0, 0, tiled=True)
    fine_result, middle_result = call(
        final_kernel, "final", [like(own.shape, jnp.bfloat16), like(middle.shape, jnp.bfloat16)],
        pinned(own), aggregate,
        *map(pinned, (node_in, row(node_bias), node_out, row(node_bias_two), row(node_gain))),
        middle_mid, from_owners,
        *map(pinned, (mid_parents, mid_weights, fine_parent, fine_weight)), coarse_own=coarse_own,
    )
    return (
        fine_result.reshape(fine_nodes.shape),
        edge_result.reshape(edge_states.shape),
        middle_result.reshape(middle_nodes.shape),
        coarse_result,
    )


def solution(mesh):
    placed = (
        P("gx", "gy", None, None),
        P("gx", "gy", None, None, None),
        P("gx", "gy", None, None),
        P(("gx", "gy"), None),
        P("gx", "gy", None, None),
        P("gx", "gy", None),
        P("gx", "gy", None, None),
        P("gx", "gy"),
        P("gx", "gy", None),
        P("gx", "gy", None),
        P("gx", "gy", None),
        P("gx", "gy", None),
        P(),
        P(),
        P(),
        P(),
        P(),
        P(),
        P(),
        P(),
        P(),
        P(),
        P(),
        P(),
        P(),
        P(),
        P(),
    )
    return jax.shard_map(
        body,
        mesh=mesh,
        in_specs=placed,
        out_specs=(
            P("gx", "gy", None, None),
            P("gx", "gy", None, None, None),
            P("gx", "gy", None, None),
            P(("gx", "gy"), None),
        ),
        check_vma=False,
    )
```
